256 devices in a mesh: train: 32 (over z, y_lo, core), pre: 8 (over x, y_hi).
Axes of the slice: x: 4, y: 4 (y_hi: 2, y_lo: 2; y = y_hi * 2 + y_lo), z: 8, core: 2. Of those that a mesh axis runs over, the one named last changes fastest.
Arguments:
- gradient: float32 [256, 512, 512], P('pre', 'train'), may hold values from -720 to 720
- assignment: int32 [8, 32], P('pre'), may hold values from 0 to 31, each once within a row
- left_prev: float32 [8, 32, 512, 512], P('pre', 'train'), may hold values from -2 to 3072, as said below
- right_prev: float32 [8, 32, 512, 512], P('pre', 'train'), may hold values from -2 to 3072, as said below
Outputs:
- update: float32 [256, 512, 512], P('pre', 'train')
- left_root: float32 [256, 512, 512], P('pre', 'train')
- right_root: float32 [256, 512, 512], P('pre', 'train')
- left_stat: float32 [8, 32, 512, 512], P('pre', 'train')
- right_stat: float32 [8, 32, 512, 512], P('pre', 'train')
The draws below stay inside these ranges and needn't reach their ends.
Inputs may be any that keep to these rules, and one draw needn't show every extreme that they name: `assignment`: each row lists every block number of its group once. `left_prev`: each block is symmetric and positive definite. `right_prev`: each block is symmetric and positive definite.
All inputs are finite; a program needn't handle non-finite values.
Results may differ from the reference program's by a relative error of at most 0.0095.
The reference program's roundings to bfloat16 on the way count: a program that leaves them out, or rounds other values in their place, can miss the bound.
Values sent between devices are 32-bit elements; how exact they have to be, the bound alone decides.
A program may use at most 64 MiB of HBM per device.

```python
import math
import jax
import jax.numpy as jnp
from jax import lax

B = 512
ITERS = 3
GROUPS = 8
NBG = 32
NBLK = 256


def draw_gradient(key, part):
    key = jax.random.fold_in(key, 11)
    subkeys = jax.random.split(key, 4)
    positions = jnp.arange(B, dtype=jnp.float32)
    row_scale = jnp.exp(jax.random.uniform(subkeys[0], (B,), minval=0.0, maxval=math.log(10.0))) * 3.0 ** (positions / B)
    col_scale = jnp.exp(jax.random.uniform(subkeys[1], (B,), minval=0.0, maxval=math.log(10.0)))
    block_index = jnp.arange(NBLK, dtype=jnp.float32)
    block_scale = 3.0 ** (block_index / NBLK) * jnp.exp(jax.random.uniform(subkeys[2], (NBLK,), minval=0.0, maxval=math.log(2.0)))
    noise_base = jnp.clip(jax.random.normal(subkeys[3], (NBLK, B, B)), -4.0, 4.0)
    return 0.1 * noise_base * block_scale[:, None, None] * row_scale[None, :, None] * col_scale[None, None, :]


def draw_left_prev(key, part):
    key = jax.random.fold_in(key, 23)
    subkeys = jax.random.split(key, 2)
    upper_part = jax.random.uniform(subkeys[0], (GROUPS, NBG, B, B), minval=-2.0, maxval=2.0)
    positions = jnp.arange(B)
    above_diagonal = positions[:, None] < positions[None, :]
    off_part = jnp.where(above_diagonal, upper_part, jnp.swapaxes(upper_part, -1, -2))
    diagonal = jnp.exp(jax.random.uniform(subkeys[1], (GROUPS, NBG, B), minval=math.log(2.0 * B), maxval=math.log(6.0 * B)))
    on_diagonal = positions[:, None] == positions[None, :]
    return jnp.where(on_diagonal, diagonal[..., :, None], off_part)


def draw_right_prev(key, part):
    key = jax.random.fold_in(key, 37)
    subkeys = jax.random.split(key, 2)
    upper_part = jax.random.uniform(subkeys[0], (GROUPS, NBG, B, B), minval=-2.0, maxval=2.0)
    positions = jnp.arange(B)
    above_diagonal = positions[:, None] < positions[None, :]
    off_part = jnp.where(above_diagonal, upper_part, jnp.swapaxes(upper_part, -1, -2))
    diagonal = jnp.exp(jax.random.uniform(subkeys[1], (GROUPS, NBG, B), minval=math.log(2.0 * B), maxval=math.log(6.0 * B)))
    on_diagonal = positions[:, None] == positions[None, :]
    return jnp.where(on_diagonal, diagonal[..., :, None], off_part)


def setup_inputs(seed: int = 0) -> dict:
    key_of = jax.random.split(jax.random.key(seed), 5)
    return {
        "gradient": draw_gradient(jax.random.fold_in(key_of[4], 71), 0),
        "assignment": jax.vmap(lambda own: jax.random.permutation(own, NBG))(jax.random.split(key_of[1], GROUPS)).reshape((GROUPS, NBG)).astype(jnp.int32),
        "left_prev": draw_left_prev(jax.random.fold_in(key_of[4], 71), 0),
        "right_prev": draw_right_prev(jax.random.fold_in(key_of[4], 71), 0),
    }


decay_rate = 0.95
highest = lax.Precision.HIGHEST

def full_product(left, right):
    return jnp.dot(left, right, precision=highest, preferred_element_type=jnp.float32)

def to_half(values):
    return values.astype(jnp.bfloat16)

def half_product(left, right):
    left_wide = lax.optimization_barrier(left).astype(jnp.float32)
    right_wide = lax.optimization_barrier(right).astype(jnp.float32)
    return jnp.dot(left_wide, right_wide, precision=highest, preferred_element_type=jnp.float32)

def inverse_root(statistic):
    identity = jnp.eye(statistic.shape[0], dtype=jnp.float32)
    start_scale = 2.5 / jnp.sqrt(jnp.sum(statistic * statistic))
    iterate = start_scale * statistic
    root_part = jnp.sqrt(jnp.sqrt(start_scale)) * identity
    for sweep in range(ITERS):
        factor = to_half(1.25 * identity - 0.25 * iterate)
        square = to_half(half_product(factor, factor))
        fourth = to_half(half_product(square, square))
        iterate = half_product(fourth, to_half(iterate))
        root_part = half_product(to_half(root_part), factor)
    return root_part

def owner_work(pieces):
    grad_block, left_old, right_old = pieces
    left_new = decay_rate * left_old + (1.0 - decay_rate) * full_product(grad_block, grad_block.T)
    right_new = decay_rate * right_old + (1.0 - decay_rate) * full_product(grad_block.T, grad_block)
    left_factor = inverse_root(left_new)
    right_factor = inverse_root(right_new)
    precond = full_product(left_factor, full_product(grad_block, right_factor))
    return (left_new, right_new, left_factor, right_factor, precond)

def reference(gradient, assignment, left_prev, right_prev):
    offsets = (jnp.arange(GROUPS, dtype=jnp.int32) * NBG)[:, None]
    global_index = (assignment.astype(jnp.int32) + offsets).reshape(-1)
    slot_grads = jnp.take(gradient, global_index, axis=0)
    left_new, right_new, left_factor, right_factor, precond = lax.map(owner_work, (slot_grads, left_prev.reshape(NBLK, B, B), right_prev.reshape(NBLK, B, B)))
    grad_total = jnp.sum(gradient * gradient)
    prec_total = jnp.sum(precond * precond)
    graft = jnp.sqrt(grad_total / (prec_total + 1e-06))

    def to_blocks(values):
        return jnp.zeros_like(values).at[global_index].set(values)
    return (to_blocks(precond) * graft, to_blocks(left_factor), to_blocks(right_factor), left_new.reshape(GROUPS, NBG, B, B), right_new.reshape(GROUPS, NBG, B, B))
```

```python
import jax
import jax.numpy as jnp
from jax import lax
from jax.experimental import pallas as pl
from jax.experimental.pallas import tpu as pltpu
from jax.sharding import PartitionSpec as P

MESH = pl.DeviceIdType.MESH
DECAY = 0.95
ITERS = 3
RINGS = 8
SUBS = 4


def split(values):
    high = values.astype(jnp.bfloat16)
    low = (values - high.astype(jnp.float32)).astype(jnp.bfloat16)
    return high, low


def dot(left, right):
    return jnp.dot(left, right, preferred_element_type=jnp.float32)


def dot_t(left, right):
    return lax.dot_general(
        left, right, (((1,), (1,)), ((), ())), preferred_element_type=jnp.float32
    )


def total(values):
    return jnp.sum(jnp.sum(values, axis=0, keepdims=True), axis=1, keepdims=True)


def halves(width):
    return [slice(start, start + width // 2) for start in (0, width // 2)]


def product(left, right, finish):
    for part in halves(right.shape[1]):
        finish(part, dot(left[...], right[:, part]))


def product_full(left_high, left_low, right_high, right_low, finish):
    for part in halves(right_high.shape[1]):
        cross = dot(left_high[...], right_low[:, part]) + dot(left_low[...], right_high[:, part])
        finish(part, dot(left_high[...], right_high[:, part]) + cross)


def keep(target):
    def finish(part, values):
        target[:, part] = values.astype(target.dtype)

    return finish


def put_factor(factor, part, iterate):
    for rows in halves(factor.shape[0]):
        values = -0.25 * iterate[rows]
        if rows == part:
            shape = values.shape
            diagonal = lax.broadcasted_iota(jnp.int32, shape, 0) == lax.broadcasted_iota(
                jnp.int32, shape, 1
            )
            values = jnp.where(diagonal, 1.25 + values, values)
        factor[rows, part] = values.astype(jnp.bfloat16)


def inverse_root(stat, squares, factor, square, fourth, iterate, root, finish):
    scale = 2.5 / jnp.sqrt(squares)
    start = jnp.sqrt(jnp.sqrt(scale)).astype(jnp.bfloat16).astype(jnp.float32)
    for part in halves(stat.shape[1]):
        values = scale * stat[:, part]
        iterate[0, :, part] = values.astype(jnp.bfloat16)
        put_factor(factor.at[0], part, values)
        root[0, :, part] = (start * factor[0, :, part].astype(jnp.float32)).astype(jnp.bfloat16)

    def advance(now, last):
        def finish_iterate(part, values):
            if not last:
                iterate[now + 1, :, part] = values.astype(jnp.bfloat16)
            put_factor(factor.at[now + 1], part, values)

        product(factor.at[now], factor.at[now], keep(square))
        product(square, square, keep(fourth))
        product(fourth, iterate.at[now], finish_iterate)

    advance(0, False)
    product(root.at[0], factor.at[1], keep(root.at[1]))
    advance(1, True)
    product(root.at[1], factor.at[2], finish)


def body(
    order_hbm, grad_hbm, left_prev, right_prev,
    precond_in, left_root_hbm, right_root_hbm, left_stat_hbm, right_stat_hbm, norm_hbm,
    grad, outgoing, owned, left_old, right_old, left_new, right_new,
    left, right, precond, left_in, right_in, ready,
    high, low, other_high, other_low, factor, square, fourth, iterate, root,
    norm, norm_group, norm_all, norm_pre, norm_train, order, place,
    in_sems, out_sems, send_sems, recv_grad, recv_sems, norm_send, norm_recv,
):
    me, group = lax.axis_index("train"), lax.axis_index("pre")
    n, groups = lax.axis_size("train"), lax.axis_size("pre")
    blocks, rows, width = grad.shape
    plane, y_at, core_at = me // SUBS, (me // 2) % 2, me % 2

    barrier = pltpu.get_barrier_semaphore()

    load_left = pltpu.make_async_copy(left_prev, left_old, in_sems.at[1])
    load_right = pltpu.make_async_copy(right_prev, right_old, in_sems.at[2])
    load_order = pltpu.make_async_copy(order_hbm, order, in_sems.at[3])
    load_order.start()
    load_grad = copy_in_parts(grad_hbm, grad, in_sems.at[pl.ds(4, 4)])
    load_left.start()
    load_right.start()
    def greet_train(k, _):
        pl.semaphore_signal(
            barrier, inc=1, device_id={"train": (me + k) % n}, device_id_type=MESH
        )
        return 0

    def greet_pre(k, _):
        pl.semaphore_signal(
            barrier, inc=1, device_id={"pre": (group + k) % groups}, device_id_type=MESH
        )
        return 0

    lax.fori_loop(1, n, greet_train, 0)

    @pl.when(me == 0)
    def _():
        lax.fori_loop(1, groups, greet_pre, 0)

    load_order.wait()
    for load in load_grad:
        load.wait()

    def pick(slot, _):
        outgoing[slot] = grad[order[0, slot]]
        return 0

    lax.fori_loop(0, n, pick, 0)
    pl.semaphore_wait(barrier, n - 1 + jnp.where(me == 0, groups - 1, 0))

    def offset(half, k, core):
        step = half * (RINGS // 2) + k % (RINGS // 2)
        way = (2 * (step % 2) - 1) * (1 - 2 * core)
        return (RINGS - step) // 2 * way, (step + k // (RINGS // 2) + 2) % SUBS

    def device_at(dz, sub):
        z = (plane + dz + RINGS) % RINGS
        return (z * 2 + (y_at + sub // 2) % 2) * 2 + (core_at + sub) % 2

    def push(source, target, send_sem, recv_sem, other):
        pltpu.make_async_remote_copy(
            src_ref=source,
            dst_ref=target,
            send_sem=send_sem,
            recv_sem=recv_sem,
            device_id={"train": other},
            device_id_type=MESH,
        ).start()

    def send_grad(core, half, some=None):
        def send(j, _):
            if some is None:
                step, across = half * (RINGS // 2) + j // 2, (j + 1) % 2
            else:
                step = half * (RINGS // 2) + j
                across = (plane + (RINGS - step) // 2 + y_at + some) % 2
            sub = 2 * across + (core_at + core) % 2
            slot = (sub - step + 10) % SUBS * SUBS + step % (RINGS // 2)
            dz, _ = offset(half, slot, core_at)
            other = device_at(dz, sub)
            at = half * (n // 2) + slot
            push(outgoing.at[other], owned.at[at], send_sems.at[0], recv_grad.at[half], other)
            return 0

        own = core_at == core
        if some is not None:
            own &= (plane + y_at) % 2 == some
        count = RINGS if some is None else RINGS // 2
        lax.fori_loop(0, count - half * jnp.where(own, 1, 0), send, 0)

    def send_half(source, target, which, half):
        def send(k, _):
            other = device_at(*offset(half, k, core_at))
            push(source.at[other], target.at[me], send_sems.at[which], recv_sems.at[which], other)
            return 0

        lax.fori_loop(0, n // 2 - half, send, 0)

    def send_all(source, target, which):
        send_half(source, target, which, 0)
        send_half(source, target, which, 1)

    def wait_bytes(ref, sem, count=n - 1):
        some = ref.at[pl.ds(0, count)]
        pltpu.make_async_copy(some, some, sem).wait()

    for core, some in ((0, None), (1, 0), (1, 1)):
        for half in range(2):
            send_grad(core, half, some)
    owned[n - 1] = outgoing[me]

    def invert(block, _):
        def look(slot, found):
            return jnp.where(order[0, slot] == block, slot, found)

        place[block] = lax.fori_loop(0, n, look, 0)
        return 0

    lax.fori_loop(0, blocks, invert, 0)
    grad_sum = total(jnp.sum(grad[...] * grad[...], axis=0))

    def whole(values, count=n):
        return values.reshape(count * rows, width)

    def gram_of(half):
        count = n // 2
        some_high, some_low = split(whole(owned[half * count : (half + 1) * count], count))
        turned_high, turned_low = some_high.T, some_low.T
        for part in halves(width):
            cross = dot(turned_high, some_low[:, part]) + dot(turned_low, some_high[:, part])
            yield part, dot(turned_high, some_high[:, part]) + cross

    def keep_stat(stat, parts):
        squares = jnp.zeros((1, width // 2), jnp.float32)
        for part, values in parts:
            stat[:, part] = values
            squares += jnp.sum(values * values, axis=0, keepdims=True)
        return jnp.sum(squares, axis=1, keepdims=True)

    def put_root(stat, squares, target):
        def finish(part, values):
            target[:, :, part] = values.reshape(n, rows, width // 2)

        inverse_root(stat, squares, factor, square, fourth, iterate, root, finish)

    load_right.wait()
    wait_bytes(owned, recv_grad.at[0], n // 2)
    for part, gram in gram_of(0):
        right_new[:, part] = DECAY * right_old[:, part] + (1.0 - DECAY) * gram
    wait_bytes(owned.at[pl.ds(n // 2, n // 2)], recv_grad.at[1], n // 2 - 1)
    squares = keep_stat(
        right_new,
        [
            (part, right_new[:, part] + (1.0 - DECAY) * gram)
            for part, gram in gram_of(1)
        ],
    )
    store_right_stat = pltpu.make_async_copy(right_new, right_stat_hbm, out_sems.at[1])
    store_right_stat.start()
    put_root(right_new, squares, right)
    send_all(right, right_in, 1)
    right_in[me] = right[me]

    def place_rows(k, _):
        half, slot = k // (n // 2), k % (n // 2)
        _, sub = offset(half, slot, 0)
        dz, _ = offset(half, slot, (core_at + sub) % 2)
        at = pl.ds(pl.multiple_of(device_at(-dz, sub) * rows, rows), rows)
        high[at], low[at] = split(owned[k])
        return 0

    lax.fori_loop(0, n, place_rows, 0)
    load_left.wait()
    parts = []
    for part in halves(width):
        gram = dot_t(high[...], high[part]) + (
            dot_t(high[...], low[part]) + dot_t(low[...], high[part])
        )
        parts.append((part, DECAY * left_old[:, part] + (1.0 - DECAY) * gram))
    squares = keep_stat(left_new, parts)
    store_left_stat = pltpu.make_async_copy(left_new, left_stat_hbm, out_sems.at[0])
    store_left_stat.start()
    put_root(left_new, squares, left)
    left_in[me] = left[me]

    def keep_split(part, values):
        right_old[:, part] = values

    other_high[...], other_low[...] = split(whole(right[...]))
    product_full(high, low, other_high, other_low, keep_split)
    high[...], low[...] = split(right_old[...])
    other_high[...], other_low[...] = split(whole(left[...]))

    def keep_precond(part, values):
        precond[:, :, part] = values.reshape(n, rows, width // 2)

    product_full(other_high, other_low, high, low, keep_precond)
    prec_sum = total(jnp.sum(precond[...] * precond[...], axis=0))
    upper = lax.broadcasted_iota(jnp.int32, norm.shape, 0) < 4
    norm[...] = jnp.where(upper, grad_sum, prec_sum)

    def share(source, target, which, device):
        pltpu.make_async_remote_copy(
            src_ref=source,
            dst_ref=target,
            send_sem=norm_send.at[which],
            recv_sem=norm_recv.at[which],
            device_id=device,
            device_id_type=MESH,
        ).start()

    def share_pre(k, _):
        share(norm_group, norm_pre.at[group], 1, {"pre": (group + k) % groups})
        return 0

    def share_train(k, _):
        share(norm_all, norm_all, 2, {"train": k})
        return 0

    @pl.when(me != 0)
    def _():
        share(norm, norm_train.at[me], 0, {"train": 0})

    send_all(left, left_in, 2)

    @pl.when(me == 0)
    def _():
        norm_train[0] = norm[...]
        wait_bytes(norm_train, norm_recv.at[0])
        norm_group[...] = jnp.sum(norm_train[...], axis=0)
        lax.fori_loop(1, groups, share_pre, 0)
        norm_pre[group] = norm_group[...]

    send_half(precond, precond_in, 3, 0)

    @pl.when(me == 0)
    def _():
        wait_bytes(norm_pre, norm_recv.at[1], groups - 1)
        wait_bytes(norm_pre, norm_send.at[1], groups - 1)
        norm_all[...] = jnp.sum(norm_pre[...], axis=0)
        lax.fori_loop(1, n, share_train, 0)

    send_half(precond, precond_in, 3, 1)
    keep_own = pltpu.make_async_copy(precond.at[me], precond_in.at[me], out_sems.at[4])
    keep_own.start()

    def to_blocks(source, target, which):
        def move(block, _):
            ready[which, block] = source[place[block]]
            return 0

        lax.fori_loop(0, blocks, move, 0)
        store = pltpu.make_async_copy(ready.at[which], target, out_sems.at[2 + which])
        store.start()
        return store

    wait_bytes(right_in, recv_sems.at[1])
    store_right = to_blocks(right_in, right_root_hbm, 1)
    wait_bytes(left_in, recv_sems.at[2])
    store_left = to_blocks(left_in, left_root_hbm, 0)

    @pl.when(me != 0)
    def _():
        pltpu.make_async_copy(norm, norm, norm_send.at[0]).wait()
        pltpu.make_async_copy(norm_all, norm_all, norm_recv.at[2]).wait()

    @pl.when(me == 0)
    def _():
        wait_bytes(norm_train, norm_send.at[2])

    store_norm = pltpu.make_async_copy(norm_all, norm_hbm, out_sems.at[5])
    store_norm.start()
    wait_bytes(owned, send_sems.at[0])
    wait_bytes(right, send_sems.at[1])
    wait_bytes(left, send_sems.at[2])
    wait_bytes(precond, send_sems.at[3])
    store_left_stat.wait()
    store_right_stat.wait()
    store_left.wait()
    store_right.wait()
    store_norm.wait()
    keep_own.wait()
    wait_bytes(precond_in, recv_sems.at[3])


def in_hbm(value):
    return pltpu.with_memory_space_constraint(value, pltpu.HBM)


def copy_in_parts(source, target, sems):
    count = source.shape[0] // 4
    parts = [pl.ds(part * count, count) for part in range(4)]
    copies = [
        pltpu.make_async_copy(source.at[at], target.at[at], sems.at[part])
        for part, at in enumerate(parts)
    ]
    for copy in copies:
        copy.start()
    return copies


def deliver(
    order_hbm, precond_hbm, left, right, left_stat, right_stat, norm_hbm,
    update, left_out, right_out, left_stat_out, right_stat_out,
    precond, norm, order, in_sems, out_sems,
):
    blocks = precond.shape[0]
    load_order = pltpu.make_async_copy(order_hbm, order, in_sems.at[4])
    load_norm = pltpu.make_async_copy(norm_hbm, norm, in_sems.at[5])
    load_order.start()
    load_norm.start()
    loads = copy_in_parts(precond_hbm, precond, in_sems)
    pairs = ((left, left_out), (right, right_out), (left_stat, left_stat_out), (right_stat, right_stat_out))
    stores = []
    for i, (source, target) in enumerate(pairs):
        stores += copy_in_parts(source, target, out_sems.at[pl.ds(4 * i, 4)])
    load_order.wait()
    load_norm.wait()
    graft = jnp.sqrt(norm[0:1, 0:1] / (norm[4:5, 0:1] + 1e-6))

    def scale(slot, _):
        precond[slot] = precond[slot] * graft
        pltpu.make_async_copy(
            precond.at[slot], update.at[order[0, slot]], out_sems.at[16]
        ).start()
        return 0

    for part, load in enumerate(loads):
        load.wait()
        lax.fori_loop(part * (blocks // 4), (part + 1) * (blocks // 4), scale, 0)
    for store in stores:
        store.wait()
    pltpu.make_async_copy(precond, update, out_sems.at[16]).wait()


def shards(gradient, assignment, left_prev, right_prev):
    n, groups = lax.axis_size("train"), lax.axis_size("pre")
    blocks, rows, width = gradient.shape
    pieces = jax.ShapeDtypeStruct((blocks, rows, width), jnp.float32)
    square = jax.ShapeDtypeStruct((width, width), jnp.float32)
    any_space = pl.BlockSpec(memory_space=pl.ANY)
    pieces_vmem = pltpu.VMEM(pieces.shape, jnp.float32)
    square_vmem = pltpu.VMEM(square.shape, jnp.float32)
    square_half = pltpu.VMEM(square.shape, jnp.bfloat16)
    results = (pieces, pieces, pieces, square, square)
    made = pl.pallas_call(
        body,
        out_shape=results + (jax.ShapeDtypeStruct((8, 128), jnp.float32),),
        in_specs=[pl.BlockSpec(memory_space=pltpu.HBM)] * 4,
        out_specs=(any_space,) * 6,
        scratch_shapes=[pieces_vmem] * 3
        + [square_vmem] * 4
        + [pieces_vmem] * 5
        + [
            pltpu.VMEM((2,) + pieces.shape, jnp.float32),
        ]
        + [square_half] * 4
        + [
            pltpu.VMEM((ITERS,) + square.shape, jnp.bfloat16),
            square_half,
            square_half,
            pltpu.VMEM((ITERS - 1,) + square.shape, jnp.bfloat16),
            pltpu.VMEM((ITERS - 1,) + square.shape, jnp.bfloat16),
            pltpu.VMEM((8, 128), jnp.float32),
            pltpu.VMEM((8, 128), jnp.float32),
            pltpu.VMEM((8, 128), jnp.float32),
            pltpu.VMEM((groups, 8, 128), jnp.float32),
            pltpu.VMEM((n, 8, 128), jnp.float32),
            pltpu.SMEM((1, blocks), jnp.int32),
            pltpu.SMEM((blocks,), jnp.int32),
            pltpu.SemaphoreType.DMA((8,)),
            pltpu.SemaphoreType.DMA((6,)),
            pltpu.SemaphoreType.DMA((4,)),
            pltpu.SemaphoreType.DMA((2,)),
            pltpu.SemaphoreType.DMA((4,)),
            pltpu.SemaphoreType.DMA((3,)),
            pltpu.SemaphoreType.DMA((3,)),
        ],
        compiler_params=pltpu.CompilerParams(
            collective_id=0, has_side_effects=True, vmem_limit_bytes=48 * 2**20
        ),
        cost_estimate=pl.CostEstimate(
            flops=2 * 28 * width**3, bytes_accessed=32 * width**2, transcendentals=0
        ),
        name="shampoo",
    )(*(in_hbm(value) for value in (assignment, gradient, left_prev[0, 0], right_prev[0, 0])))
    update, left_root, right_root, left_stat, right_stat = pl.pallas_call(
        deliver,
        out_shape=results,
        in_specs=[any_space] * 7,
        out_specs=(pl.BlockSpec(memory_space=pltpu.HBM),) * 5,
        scratch_shapes=[
            pieces_vmem,
            pltpu.VMEM((8, 128), jnp.float32),
            pltpu.SMEM((1, blocks), jnp.int32),
            pltpu.SemaphoreType.DMA((6,)),
            pltpu.SemaphoreType.DMA((17,)),
        ],
        compiler_params=pltpu.CompilerParams(vmem_limit_bytes=4 * 2**20),
        name="deliver",
    )(in_hbm(assignment), *made)
    return update, left_root, right_root, left_stat[None, None], right_stat[None, None]


def solution(mesh):
    by_rows = P("pre", "train", None)
    by_owner = P("pre", "train", None, None)
    return jax.shard_map(
        shards,
        mesh=mesh,
        in_specs=(by_rows, P("pre", None), by_owner, by_owner),
        out_specs=(by_rows, by_rows, by_rows, by_owner, by_owner),
        check_vma=False,
    )
```

```python
import jax
import jax.numpy as jnp
from jax import lax
from jax.experimental import pallas as pl
from jax.experimental.pallas import tpu as pltpu
from jax.sharding import PartitionSpec as P

MESH = pl.DeviceIdType.MESH
DECAY = 0.95
ITERS = 3
RINGS = 8
SUBS = 4
PAIRS = 4


def split(values):
    high = values.astype(jnp.bfloat16)
    low = (values - high.astype(jnp.float32)).astype(jnp.bfloat16)
    return high, low


def dot(left, right):
    return jnp.dot(left, right, preferred_element_type=jnp.float32)


def dot_t(left, right):
    return lax.dot_general(
        left, right, (((1,), (1,)), ((), ())), preferred_element_type=jnp.float32
    )


def total(values):
    return jnp.sum(jnp.sum(values, axis=0, keepdims=True), axis=1, keepdims=True)


def halves(width):
    return [slice(start, start + width // 2) for start in (0, width // 2)]


def product(left, right, finish):
    for part in halves(right.shape[1]):
        finish(part, dot(left[...], right[:, part]))


def product_full(left_high, left_low, right_high, right_low, finish):
    for part in halves(right_high.shape[1]):
        cross = dot(left_high[...], right_low[:, part]) + dot(left_low[...], right_high[:, part])
        finish(part, dot(left_high[...], right_high[:, part]) + cross)


def keep(target):
    def finish(part, values):
        target[:, part] = values.astype(target.dtype)

    return finish


def put_factor(factor, part, iterate):
    for rows in halves(factor.shape[0]):
        values = -0.25 * iterate[rows]
        if rows == part:
            shape = values.shape
            diagonal = lax.broadcasted_iota(jnp.int32, shape, 0) == lax.broadcasted_iota(
                jnp.int32, shape, 1
            )
            values = jnp.where(diagonal, 1.25 + values, values)
        factor[rows, part] = values.astype(jnp.bfloat16)


def inverse_root(stat, squares, factor, square, fourth, iterate, root, finish):
    scale = 2.5 / jnp.sqrt(squares)
    start = jnp.sqrt(jnp.sqrt(scale)).astype(jnp.bfloat16).astype(jnp.float32)
    for part in halves(stat.shape[1]):
        values = scale * stat[:, part]
        iterate[0, :, part] = values.astype(jnp.bfloat16)
        put_factor(factor.at[0], part, values)
        root[0, :, part] = (start * factor[0, :, part].astype(jnp.float32)).astype(jnp.bfloat16)

    def advance(now, last):
        def finish_iterate(part, values):
            if not last:
                iterate[now + 1, :, part] = values.astype(jnp.bfloat16)
            put_factor(factor.at[now + 1], part, values)

        product(factor.at[now], factor.at[now], keep(square))
        product(square, square, keep(fourth))
        product(fourth, iterate.at[now], finish_iterate)

    advance(0, False)
    product(root.at[0], factor.at[1], keep(root.at[1]))
    advance(1, True)
    product(root.at[1], factor.at[2], finish)


def body(
    order_hbm, grad_hbm, left_prev, right_prev,
    precond_in, left_root_hbm, right_root_hbm, left_stat_hbm, right_stat_hbm, norm_hbm,
    grad, outgoing, owned, left_old, right_old, left_new, right_new,
    left, right, precond, left_in, right_in, ready, turned, crossed,
    high, low, other_high, other_low, factor, square, fourth, iterate, root,
    norm, norm_group, norm_all, norm_pre, norm_train, order, place,
    in_sems, out_sems, send_sems, recv_grad, recv_sems,
    cross_send, cross_recv, norm_send, norm_recv,
):
    me, group = lax.axis_index("train"), lax.axis_index("pre")
    n, groups = lax.axis_size("train"), lax.axis_size("pre")
    blocks, rows, width = grad.shape
    plane, y_at, core_at = me // SUBS, (me // 2) % 2, me % 2
    pair, upper_plane, peers = plane // 2, plane % 2, n // PAIRS
    tile = width // PAIRS

    barrier = pltpu.get_barrier_semaphore()

    load_left = pltpu.make_async_copy(left_prev, left_old, in_sems.at[1])
    load_right = pltpu.make_async_copy(right_prev, right_old, in_sems.at[2])
    load_order = pltpu.make_async_copy(order_hbm, order, in_sems.at[3])
    load_order.start()
    load_grad = copy_in_parts(grad_hbm, grad, in_sems.at[pl.ds(4, 4)])
    load_left.start()
    load_right.start()
    def greet_train(k, _):
        pl.semaphore_signal(
            barrier, inc=1, device_id={"train": (me + k) % n}, device_id_type=MESH
        )
        return 0

    def greet_pre(k, _):
        pl.semaphore_signal(
            barrier, inc=1, device_id={"pre": (group + k) % groups}, device_id_type=MESH
        )
        return 0

    lax.fori_loop(1, n, greet_train, 0)

    @pl.when(me == 0)
    def _():
        lax.fori_loop(1, groups, greet_pre, 0)

    load_order.wait()
    for load in load_grad:
        load.wait()

    def pick(slot, _):
        outgoing[slot] = grad[order[0, slot]]
        return 0

    lax.fori_loop(0, n, pick, 0)
    pl.semaphore_wait(barrier, n - 1 + jnp.where(me == 0, groups - 1, 0))

    def offset(half, k, core):
        step = half * (RINGS // 2) + k % (RINGS // 2)
        way = (2 * (step % 2) - 1) * (1 - 2 * core)
        return (RINGS - step) // 2 * way, (step + k // (RINGS // 2) + 2) % SUBS

    def device_at(dz, sub):
        z = (plane + dz + RINGS) % RINGS
        return (z * 2 + (y_at + sub // 2) % 2) * 2 + (core_at + sub) % 2

    def push(source, target, send_sem, recv_sem, other):
        pltpu.make_async_remote_copy(
            src_ref=source,
            dst_ref=target,
            send_sem=send_sem,
            recv_sem=recv_sem,
            device_id={"train": other},
            device_id_type=MESH,
        ).start()

    def send_grad(core, half):
        def send(j, _):
            step, sub = half * (RINGS // 2) + j // 2, 2 * ((j + 1) % 2) + (core_at + core) % 2
            slot = (sub - step + 10) % SUBS * SUBS + step % (RINGS // 2)
            dz, _ = offset(half, slot, core_at)
            other = device_at(dz, sub)
            at = half * (n // 2) + slot
            push(outgoing.at[other], owned.at[at], send_sems.at[0], recv_grad.at[half], other)
            return 0

        lax.fori_loop(0, RINGS - half * jnp.where(core_at == core, 1, 0), send, 0)

    def send_half(source, target, which, half):
        def send(k, _):
            other = device_at(*offset(half, k, core_at))
            push(source.at[other], target.at[me], send_sems.at[which], recv_sems.at[which], other)
            return 0

        lax.fori_loop(0, n // 2 - half, send, 0)

    def columns(which_pair):
        return pl.ds(pl.multiple_of(which_pair % PAIRS * tile, tile), tile)

    def send_root(source, target, which):
        send_sem, recv_sem = send_sems.at[which], recv_sems.at[which]

        def send_tiles(k, _):
            place = k // (PAIRS - 1)
            other = (pair + 2) % PAIRS * peers + place
            skipped = pair + 1 + 2 * (place // SUBS)
            at = columns(skipped + 1 + k % (PAIRS - 1))
            push(source.at[other, :, at], target.at[me, :, at], send_sem, recv_sem, other)
            return 0

        def send(k, _):
            step = k % 6
            dz = (6 - step) // 2 * (1 - 2 * (step % 2)) * (1 - 2 * upper_plane)
            other = device_at(dz, (step + k // 6) % SUBS)
            push(source.at[other], target.at[me], send_sem, recv_sem, other)
            return 0

        lax.fori_loop(0, peers * (PAIRS - 1), send_tiles, 0)
        lax.fori_loop(0, n - peers - 1, send, 0)
        target[me] = source[me]

    root_chunks = n - peers - 1 + peers * (PAIRS - 1) // PAIRS

    def exchange(target, which):
        for way in range(2):
            to = (pair + 1 + 2 * way) % PAIRS
            owners = (to + 2) % PAIRS * peers
            held = target[pl.ds(owners, peers), :, columns(to)].reshape(peers * rows, tile)
            part = held.T[way * SUBS * rows : (way + 1) * SUBS * rows]
            turned[which, way] = part.reshape(SUBS, rows, tile)

            def send(k, _):
                other = to * peers + way * SUBS + k
                push(
                    turned.at[which, way, k], crossed.at[which, me % peers],
                    cross_send.at[which], cross_recv.at[which], other,
                )
                return 0

            lax.fori_loop(0, SUBS, send, 0)

    def place_crossed(target, which):
        arrived = crossed.at[which]
        pltpu.make_async_copy(arrived, arrived, cross_recv.at[which]).wait()
        at = columns(pair + 3 + 2 * upper_plane)
        owners = (pair + 2) % PAIRS * peers
        lane = lax.broadcasted_iota(jnp.int32, (rows, tile), 1) // rows
        pieces = [crossed[which, sender] for sender in range(peers)]
        for block in range(peers):
            values = jnp.zeros((rows, tile), jnp.float32)
            for sender in range(peers):
                shift = (sender - block) % peers * rows
                moved = pltpu.roll(pieces[sender], shift, 1) if shift else pieces[sender]
                values = jnp.where(lane == sender, moved, values)
            target[owners + block, :, at] = values

    def wait_bytes(ref, sem, count=n - 1):
        some = ref.at[pl.ds(0, count)]
        pltpu.make_async_copy(some, some, sem).wait()

    for core in range(2):
        for half in range(2):
            send_grad(core, half)
    owned[n - 1] = outgoing[me]

    def invert(block, _):
        def look(slot, found):
            return jnp.where(order[0, slot] == block, slot, found)

        place[block] = lax.fori_loop(0, n, look, 0)
        return 0

    lax.fori_loop(0, blocks, invert, 0)
    grad_sum = total(jnp.sum(grad[...] * grad[...], axis=0))

    def whole(values, count=n):
        return values.reshape(count * rows, width)

    def gram_of(half):
        count = n // 2
        some_high, some_low = split(whole(owned[half * count : (half + 1) * count], count))
        turned_high, turned_low = some_high.T, some_low.T
        for part in halves(width):
            cross = dot(turned_high, some_low[:, part]) + dot(turned_low, some_high[:, part])
            yield part, dot(turned_high, some_high[:, part]) + cross

    def keep_stat(stat, parts):
        squares = jnp.zeros((1, width // 2), jnp.float32)
        for part, values in parts:
            stat[:, part] = values
            squares += jnp.sum(values * values, axis=0, keepdims=True)
        return jnp.sum(squares, axis=1, keepdims=True)

    def put_root(stat, squares, target):
        def finish(part, values):
            target[:, :, part] = values.reshape(n, rows, width // 2)

        inverse_root(stat, squares, factor, square, fourth, iterate, root, finish)

    load_right.wait()
    wait_bytes(owned, recv_grad.at[0], n // 2)
    for part, gram in gram_of(0):
        right_new[:, part] = DECAY * right_old[:, part] + (1.0 - DECAY) * gram
    wait_bytes(owned.at[pl.ds(n // 2, n // 2)], recv_grad.at[1], n // 2 - 1)
    squares = keep_stat(
        right_new,
        [
            (part, right_new[:, part] + (1.0 - DECAY) * gram)
            for part, gram in gram_of(1)
        ],
    )
    store_right_stat = pltpu.make_async_copy(right_new, right_stat_hbm, out_sems.at[1])
    store_right_stat.start()
    put_root(right_new, squares, right)
    send_root(right, right_in, 1)

    def place_rows(k, _):
        half, slot = k // (n // 2), k % (n // 2)
        _, sub = offset(half, slot, 0)
        dz, _ = offset(half, slot, (core_at + sub) % 2)
        at = pl.ds(pl.multiple_of(device_at(-dz, sub) * rows, rows), rows)
        high[at], low[at] = split(owned[k])
        return 0

    lax.fori_loop(0, n, place_rows, 0)
    load_left.wait()
    parts = []
    for part in halves(width):
        gram = dot_t(high[...], high[part]) + (
            dot_t(high[...], low[part]) + dot_t(low[...], high[part])
        )
        parts.append((part, DECAY * left_old[:, part] + (1.0 - DECAY) * gram))
    squares = keep_stat(left_new, parts)
    store_left_stat = pltpu.make_async_copy(left_new, left_stat_hbm, out_sems.at[0])
    store_left_stat.start()
    put_root(left_new, squares, left)

    def keep_split(part, values):
        right_old[:, part] = values

    other_high[...], other_low[...] = split(whole(right[...]))
    product_full(high, low, other_high, other_low, keep_split)
    high[...], low[...] = split(right_old[...])
    other_high[...], other_low[...] = split(whole(left[...]))

    def keep_precond(part, values):
        precond[:, :, part] = values.reshape(n, rows, width // 2)

    product_full(other_high, other_low, high, low, keep_precond)
    prec_sum = total(jnp.sum(precond[...] * precond[...], axis=0))
    upper = lax.broadcasted_iota(jnp.int32, norm.shape, 0) < 4
    norm[...] = jnp.where(upper, grad_sum, prec_sum)

    def share(source, target, which, device):
        pltpu.make_async_remote_copy(
            src_ref=source,
            dst_ref=target,
            send_sem=norm_send.at[which],
            recv_sem=norm_recv.at[which],
            device_id=device,
            device_id_type=MESH,
        ).start()

    def share_pre(k, _):
        share(norm_group, norm_pre.at[group], 1, {"pre": (group + k) % groups})
        return 0

    def share_train(k, _):
        share(norm_all, norm_all, 2, {"train": k})
        return 0

    @pl.when(me != 0)
    def _():
        share(norm, norm_train.at[me], 0, {"train": 0})

    send_root(left, left_in, 2)

    @pl.when(me == 0)
    def _():
        norm_train[0] = norm[...]
        wait_bytes(norm_train, norm_recv.at[0])
        norm_group[...] = jnp.sum(norm_train[...], axis=0)
        lax.fori_loop(1, groups, share_pre, 0)
        norm_pre[group] = norm_group[...]

    wait_bytes(right_in, recv_sems.at[1], root_chunks)
    exchange(right_in, 0)
    send_half(precond, precond_in, 3, 0)

    @pl.when(me == 0)
    def _():
        wait_bytes(norm_pre, norm_recv.at[1], groups - 1)
        wait_bytes(norm_pre, norm_send.at[1], groups - 1)
        norm_all[...] = jnp.sum(norm_pre[...], axis=0)
        lax.fori_loop(1, n, share_train, 0)

    wait_bytes(left_in, recv_sems.at[2], root_chunks)
    exchange(left_in, 1)
    send_half(precond, precond_in, 3, 1)
    keep_own = pltpu.make_async_copy(precond.at[me], precond_in.at[me], out_sems.at[4])
    keep_own.start()

    def to_blocks(source, target, which):
        def move(block, _):
            ready[which, block] = source[place[block]]
            return 0

        lax.fori_loop(0, blocks, move, 0)
        store = pltpu.make_async_copy(ready.at[which], target, out_sems.at[2 + which])
        store.start()
        return store

    place_crossed(right_in, 0)
    store_right = to_blocks(right_in, right_root_hbm, 1)
    place_crossed(left_in, 1)
    store_left = to_blocks(left_in, left_root_hbm, 0)

    @pl.when(me != 0)
    def _():
        pltpu.make_async_copy(norm, norm, norm_send.at[0]).wait()
        pltpu.make_async_copy(norm_all, norm_all, norm_recv.at[2]).wait()

    @pl.when(me == 0)
    def _():
        wait_bytes(norm_train, norm_send.at[2])

    store_norm = pltpu.make_async_copy(norm_all, norm_hbm, out_sems.at[5])
    store_norm.start()
    wait_bytes(owned, send_sems.at[0])
    wait_bytes(right, send_sems.at[1], root_chunks)
    wait_bytes(left, send_sems.at[2], root_chunks)
    for which in range(2):
        pltpu.make_async_copy(turned.at[which], turned.at[which], cross_send.at[which]).wait()
    wait_bytes(precond, send_sems.at[3])
    store_left_stat.wait()
    store_right_stat.wait()
    store_left.wait()
    store_right.wait()
    store_norm.wait()
    keep_own.wait()
    wait_bytes(precond_in, recv_sems.at[3])


def in_hbm(value):
    return pltpu.with_memory_space_constraint(value, pltpu.HBM)


def copy_in_parts(source, target, sems):
    count = source.shape[0] // 4
    parts = [pl.ds(part * count, count) for part in range(4)]
    copies = [
        pltpu.make_async_copy(source.at[at], target.at[at], sems.at[part])
        for part, at in enumerate(parts)
    ]
    for copy in copies:
        copy.start()
    return copies


def deliver(
    order_hbm, precond_hbm, left, right, left_stat, right_stat, norm_hbm,
    update, left_out, right_out, left_stat_out, right_stat_out,
    precond, norm, order, in_sems, out_sems,
):
    blocks = precond.shape[0]
    load_order = pltpu.make_async_copy(order_hbm, order, in_sems.at[4])
    load_norm = pltpu.make_async_copy(norm_hbm, norm, in_sems.at[5])
    load_order.start()
    load_norm.start()
    loads = copy_in_parts(precond_hbm, precond, in_sems)
    pairs = ((left, left_out), (right, right_out), (left_stat, left_stat_out), (right_stat, right_stat_out))
    stores = []
    for i, (source, target) in enumerate(pairs):
        stores += copy_in_parts(source, target, out_sems.at[pl.ds(4 * i, 4)])
    load_order.wait()
    load_norm.wait()
    graft = jnp.sqrt(norm[0:1, 0:1] / (norm[4:5, 0:1] + 1e-6))

    def scale(slot, _):
        precond[slot] = precond[slot] * graft
        pltpu.make_async_copy(
            precond.at[slot], update.at[order[0, slot]], out_sems.at[16]
        ).start()
        return 0

    for part, load in enumerate(loads):
        load.wait()
        lax.fori_loop(part * (blocks // 4), (part + 1) * (blocks // 4), scale, 0)
    for store in stores:
        store.wait()
    pltpu.make_async_copy(precond, update, out_sems.at[16]).wait()


def shards(gradient, assignment, left_prev, right_prev):
    n, groups = lax.axis_size("train"), lax.axis_size("pre")
    blocks, rows, width = gradient.shape
    pieces = jax.ShapeDtypeStruct((blocks, rows, width), jnp.float32)
    square = jax.ShapeDtypeStruct((width, width), jnp.float32)
    any_space = pl.BlockSpec(memory_space=pl.ANY)
    pieces_vmem = pltpu.VMEM(pieces.shape, jnp.float32)
    square_vmem = pltpu.VMEM(square.shape, jnp.float32)
    square_half = pltpu.VMEM(square.shape, jnp.bfloat16)
    results = (pieces, pieces, pieces, square, square)
    made = pl.pallas_call(
        body,
        out_shape=results + (jax.ShapeDtypeStruct((8, 128), jnp.float32),),
        in_specs=[pl.BlockSpec(memory_space=pltpu.HBM)] * 4,
        out_specs=(any_space,) * 6,
        scratch_shapes=[pieces_vmem] * 3
        + [square_vmem] * 4
        + [pieces_vmem] * 5
        + [
            pltpu.VMEM((2,) + pieces.shape, jnp.float32),
            pltpu.VMEM((2, 2, SUBS, rows, width // PAIRS), jnp.float32),
            pltpu.VMEM((2, n // PAIRS, rows, width // PAIRS), jnp.float32),
        ]
        + [square_half] * 4
        + [
            pltpu.VMEM((ITERS,) + square.shape, jnp.bfloat16),
            square_half,
            square_half,
            pltpu.VMEM((ITERS - 1,) + square.shape, jnp.bfloat16),
            pltpu.VMEM((ITERS - 1,) + square.shape, jnp.bfloat16),
            pltpu.VMEM((8, 128), jnp.float32),
            pltpu.VMEM((8, 128), jnp.float32),
            pltpu.VMEM((8, 128), jnp.float32),
            pltpu.VMEM((groups, 8, 128), jnp.float32),
            pltpu.VMEM((n, 8, 128), jnp.float32),
            pltpu.SMEM((1, blocks), jnp.int32),
            pltpu.SMEM((blocks,), jnp.int32),
            pltpu.SemaphoreType.DMA((8,)),
            pltpu.SemaphoreType.DMA((6,)),
            pltpu.SemaphoreType.DMA((4,)),
            pltpu.SemaphoreType.DMA((2,)),
            pltpu.SemaphoreType.DMA((4,)),
            pltpu.SemaphoreType.DMA((2,)),
            pltpu.SemaphoreType.DMA((2,)),
            pltpu.SemaphoreType.DMA((3,)),
            pltpu.SemaphoreType.DMA((3,)),
        ],
        compiler_params=pltpu.CompilerParams(
            collective_id=0, has_side_effects=True, vmem_limit_bytes=48 * 2**20
        ),
        cost_estimate=pl.CostEstimate(
            flops=2 * 28 * width**3, bytes_accessed=32 * width**2, transcendentals=0
        ),
        name="shampoo",
    )(*(in_hbm(value) for value in (assignment, gradient, left_prev[0, 0], right_prev[0, 0])))
    update, left_root, right_root, left_stat, right_stat = pl.pallas_call(
        deliver,
        out_shape=results,
        in_specs=[any_space] * 7,
        out_specs=(pl.BlockSpec(memory_space=pltpu.HBM),) * 5,
        scratch_shapes=[
            pieces_vmem,
            pltpu.VMEM((8, 128), jnp.float32),
            pltpu.SMEM((1, blocks), jnp.int32),
            pltpu.SemaphoreType.DMA((6,)),
            pltpu.SemaphoreType.DMA((17,)),
        ],
        compiler_params=pltpu.CompilerParams(vmem_limit_bytes=4 * 2**20),
        name="deliver",
    )(in_hbm(assignment), *made)
    return update, left_root, right_root, left_stat[None, None], right_stat[None, None]


def solution(mesh):
    by_rows = P("pre", "train", None)
    by_owner = P("pre", "train", None, None)
    return jax.shard_map(
        shards,
        mesh=mesh,
        in_specs=(by_rows, P("pre", None), by_owner, by_owner),
        out_specs=(by_rows, by_rows, by_rows, by_owner, by_owner),
        check_vma=False,
    )
```

```python
import functools

import jax
import jax.numpy as jnp
from jax import lax
from jax.experimental import pallas as pl
from jax.experimental.pallas import tpu as pltpu
from jax.sharding import PartitionSpec as P

MESH = pl.DeviceIdType.MESH
DECAY = 0.95
ITERS = 3
RINGS = 8
SUBS = 4
PAIRS = 4


def split(values):
    high = values.astype(jnp.bfloat16)
    low = (values - high.astype(jnp.float32)).astype(jnp.bfloat16)
    return high, low


def dot(left, right):
    return jnp.dot(left, right, preferred_element_type=jnp.float32)


def dot_t(left, right):
    return lax.dot_general(
        left, right, (((1,), (1,)), ((), ())), preferred_element_type=jnp.float32
    )


def total(values):
    return jnp.sum(jnp.sum(values, axis=0, keepdims=True), axis=1, keepdims=True)


def halves(width):
    return [slice(start, start + width // 2) for start in (0, width // 2)]


def product(left, right, finish):
    for part in halves(right.shape[1]):
        finish(part, dot(left[...], right[:, part]))


def product_full(left_high, left_low, right_high, right_low, finish):
    for part in halves(right_high.shape[1]):
        cross = dot(left_high[...], right_low[:, part]) + dot(left_low[...], right_high[:, part])
        finish(part, dot(left_high[...], right_high[:, part]) + cross)


def keep(target):
    def finish(part, values):
        target[:, part] = values.astype(target.dtype)

    return finish


def put_factor(factor, part, iterate):
    for rows in halves(factor.shape[0]):
        values = -0.25 * iterate[rows]
        if rows == part:
            shape = values.shape
            diagonal = lax.broadcasted_iota(jnp.int32, shape, 0) == lax.broadcasted_iota(
                jnp.int32, shape, 1
            )
            values = jnp.where(diagonal, 1.25 + values, values)
        factor[rows, part] = values.astype(jnp.bfloat16)


def inverse_root(stat, squares, factor, square, fourth, iterate, root, finish):
    scale = 2.5 / jnp.sqrt(squares)
    start = jnp.sqrt(jnp.sqrt(scale)).astype(jnp.bfloat16).astype(jnp.float32)
    for part in halves(stat.shape[1]):
        values = scale * stat[:, part]
        iterate[0, :, part] = values.astype(jnp.bfloat16)
        put_factor(factor.at[0], part, values)
        root[0, :, part] = (start * factor[0, :, part].astype(jnp.float32)).astype(jnp.bfloat16)

    def advance(now, last):
        def finish_iterate(part, values):
            if not last:
                iterate[now + 1, :, part] = values.astype(jnp.bfloat16)
            put_factor(factor.at[now + 1], part, values)

        product(factor.at[now], factor.at[now], keep(square))
        product(square, square, keep(fourth))
        product(fourth, iterate.at[now], finish_iterate)

    advance(0, False)
    product(root.at[0], factor.at[1], keep(root.at[1]))
    advance(1, True)
    product(root.at[1], factor.at[2], finish)


def body(
    order_hbm, grad_hbm, left_prev, right_prev,
    precond_in, left_root_hbm, right_root_hbm, left_stat_hbm, right_stat_hbm, norm_hbm,
    grad, outgoing, owned, left_old, right_old, left_new, right_new,
    left, right, precond, left_in, right_in, ready, turned, crossed,
    high, low, other_high, other_low, factor, square, fourth, iterate, root,
    norm, norm_group, norm_all, norm_pre, norm_train, order, place,
    in_sems, out_sems, send_sems, recv_grad, recv_sems,
    cross_send, cross_recv, norm_send, norm_recv,
):
    me, group = lax.axis_index("train"), lax.axis_index("pre")
    n, groups = lax.axis_size("train"), lax.axis_size("pre")
    blocks, rows, width = grad.shape
    plane, y_at, core_at = me // SUBS, (me // 2) % 2, me % 2
    pair, upper_plane, peers = plane // 2, plane % 2, n // PAIRS
    tile = width // PAIRS

    barrier = pltpu.get_barrier_semaphore()

    load_left = pltpu.make_async_copy(left_prev, left_old, in_sems.at[1])
    load_right = pltpu.make_async_copy(right_prev, right_old, in_sems.at[2])
    load_order = pltpu.make_async_copy(order_hbm, order, in_sems.at[3])
    load_order.start()
    load_grad = copy_in_parts(grad_hbm, grad, in_sems.at[pl.ds(4, 4)])
    load_left.start()
    load_right.start()
    def greet_train(k, _):
        pl.semaphore_signal(
            barrier, inc=1, device_id={"train": (me + k) % n}, device_id_type=MESH
        )
        return 0

    def greet_pre(k, _):
        pl.semaphore_signal(
            barrier, inc=1, device_id={"pre": (group + k) % groups}, device_id_type=MESH
        )
        return 0

    lax.fori_loop(1, n, greet_train, 0)

    @pl.when(me == 0)
    def _():
        lax.fori_loop(1, groups, greet_pre, 0)

    load_order.wait()
    for load in load_grad:
        load.wait()

    def pick(slot, _):
        outgoing[slot] = grad[order[0, slot]]
        return 0

    lax.fori_loop(0, n, pick, 0)
    pl.semaphore_wait(barrier, n - 1 + jnp.where(me == 0, groups - 1, 0))

    def away(step, core):
        return (RINGS - step) // 2 * (2 * (step % 2) - 1) * (1 - 2 * core)

    def device_at(dz, sub):
        z = (plane + dz + RINGS) % RINGS
        return (z * 2 + (y_at + sub // 2) % 2) * 2 + (core_at + sub) % 2

    def push(source, target, send_sem, recv_sem, other):
        pltpu.make_async_remote_copy(
            src_ref=source,
            dst_ref=target,
            send_sem=send_sem,
            recv_sem=recv_sem,
            device_id={"train": other},
            device_id_type=MESH,
        ).start()

    def send_grad(core, half, step):
        across = (half + step) % 2
        other_core = (core_at + core) % 2
        other = device_at(away(step, core_at), 2 * across + other_core)
        at = half * (n // 2) + 2 * step + 1 - other_core

        @pl.when(other != me)
        def _():
            push(outgoing.at[other], owned.at[at], send_sems.at[0], recv_grad.at[half], other)

    def grad_sender(slot):
        half, step, other_core = slot // (n // 2), slot % (n // 2) // 2, 1 - slot % 2
        dz = away(step, (core_at + other_core) % 2)
        return device_at(-dz, 2 * ((half + step) % 2) + other_core)

    def send_part(source, target, which, first, last):
        def send(k, _):
            step = k % RINGS
            other = device_at(away(step, core_at), (step + k // RINGS + 2) % SUBS)
            push(source.at[other], target.at[me], send_sems.at[which], recv_sems.at[which], other)
            return 0

        lax.fori_loop(first, last, send, 0)

    def columns(which_pair):
        return pl.ds(pl.multiple_of(which_pair % PAIRS * tile, tile), tile)

    def send_root(source, target, which):
        send_sem, recv_sem = send_sems.at[which], recv_sems.at[which]

        def send_tile(k):
            place = k // (PAIRS - 1)
            other = (pair + 2) % PAIRS * peers + place
            skipped = pair + 1 + 2 * (place // SUBS)
            at = columns(skipped + 1 + k % (PAIRS - 1))
            push(source.at[other, :, at], target.at[me, :, at], send_sem, recv_sem, other)

        def send(k, _):
            send_tile(k)
            step = k % 6
            dz = (6 - step) // 2 * (1 - 2 * (step % 2)) * (1 - 2 * upper_plane)
            other = device_at(dz, (step + k // 6) % SUBS)
            push(source.at[other], target.at[me], send_sem, recv_sem, other)
            return 0

        lax.fori_loop(0, n - peers - 1, send, 0)
        send_tile(n - peers - 1)
        target[me] = source[me]

    root_chunks = n - peers - 1 + peers * (PAIRS - 1) // PAIRS

    def exchange(target, which):
        for way in range(2):
            to = (pair + 1 + 2 * way) % PAIRS
            owners = (to + 2) % PAIRS * peers
            held = target[pl.ds(owners, peers), :, columns(to)].reshape(peers * rows, tile)
            part = held.T[way * SUBS * rows : (way + 1) * SUBS * rows]
            turned[which, way] = part.reshape(SUBS, rows, tile)

            def send(k, _):
                other = to * peers + way * SUBS + k
                push(
                    turned.at[which, way, k], crossed.at[which, me % peers],
                    cross_send.at[which], cross_recv.at[which], other,
                )
                return 0

            lax.fori_loop(0, SUBS, send, 0)

    def place_crossed(target, which):
        arrived = crossed.at[which]
        pltpu.make_async_copy(arrived, arrived, cross_recv.at[which]).wait()
        at = columns(pair + 3 + 2 * upper_plane)
        owners = (pair + 2) % PAIRS * peers
        lane = lax.broadcasted_iota(jnp.int32, (rows, tile), 1) // rows
        pieces = [crossed[which, sender] for sender in range(peers)]
        for block in range(peers):
            values = jnp.zeros((rows, tile), jnp.float32)
            for sender in range(peers):
                shift = (sender - block) % peers * rows
                moved = pltpu.roll(pieces[sender], shift, 1) if shift else pieces[sender]
                values = jnp.where(lane == sender, moved, values)
            target[owners + block, :, at] = values

    def wait_bytes(ref, sem, count=n - 1):
        some = ref.at[pl.ds(0, count)]
        pltpu.make_async_copy(some, some, sem).wait()

    def send_mixed(half, first, k, _):
        for step in range(4):
            send_grad(0, half, 4 * k + step)
        send_grad(1, 0, first + k)
        return 0

    lax.fori_loop(0, 2, functools.partial(send_mixed, 0, 0), 0)
    lax.fori_loop(0, 2, functools.partial(send_mixed, 1, 2), 0)
    for half, first in ((0, 4), (1, 0)):

        def send_rest(step, _):
            send_grad(1, half, step)
            return 0

        lax.fori_loop(first, RINGS, send_rest, 0)
    owned[n - 1] = outgoing[me]

    def invert(block, _):
        def look(slot, found):
            return jnp.where(order[0, slot] == block, slot, found)

        place[block] = lax.fori_loop(0, n, look, 0)
        return 0

    lax.fori_loop(0, blocks, invert, 0)
    grad_sum = total(jnp.sum(grad[...] * grad[...], axis=0))

    def whole(values, count=n):
        return values.reshape(count * rows, width)

    def gram_of(half):
        count = n // 2
        some_high, some_low = split(whole(owned[half * count : (half + 1) * count], count))
        turned_high, turned_low = some_high.T, some_low.T
        for part in halves(width):
            cross = dot(turned_high, some_low[:, part]) + dot(turned_low, some_high[:, part])
            yield part, dot(turned_high, some_high[:, part]) + cross

    def keep_stat(stat, parts):
        squares = jnp.zeros((1, width // 2), jnp.float32)
        for part, values in parts:
            stat[:, part] = values
            squares += jnp.sum(values * values, axis=0, keepdims=True)
        return jnp.sum(squares, axis=1, keepdims=True)

    def put_root(stat, squares, target):
        def finish(part, values):
            target[:, :, part] = values.reshape(n, rows, width // 2)

        inverse_root(stat, squares, factor, square, fourth, iterate, root, finish)

    load_right.wait()
    wait_bytes(owned, recv_grad.at[0], n // 2)
    for part, gram in gram_of(0):
        right_new[:, part] = DECAY * right_old[:, part] + (1.0 - DECAY) * gram
    wait_bytes(owned.at[pl.ds(n // 2, n // 2)], recv_grad.at[1], n // 2 - 1)
    squares = keep_stat(
        right_new,
        [
            (part, right_new[:, part] + (1.0 - DECAY) * gram)
            for part, gram in gram_of(1)
        ],
    )
    store_right_stat = pltpu.make_async_copy(right_new, right_stat_hbm, out_sems.at[1])
    store_right_stat.start()
    put_root(right_new, squares, right)
    send_root(right, right_in, 1)

    def place_rows(k, _):
        at = pl.ds(pl.multiple_of(grad_sender(k) * rows, rows), rows)
        high[at], low[at] = split(owned[k])
        return 0

    lax.fori_loop(0, n, place_rows, 0)
    load_left.wait()
    parts = []
    for part in halves(width):
        gram = dot_t(high[...], high[part]) + (
            dot_t(high[...], low[part]) + dot_t(low[...], high[part])
        )
        parts.append((part, DECAY * left_old[:, part] + (1.0 - DECAY) * gram))
    squares = keep_stat(left_new, parts)
    store_left_stat = pltpu.make_async_copy(left_new, left_stat_hbm, out_sems.at[0])
    store_left_stat.start()
    put_root(left_new, squares, left)

    def keep_split(part, values):
        right_old[:, part] = values

    other_high[...], other_low[...] = split(whole(right[...]))
    product_full(high, low, other_high, other_low, keep_split)
    high[...], low[...] = split(right_old[...])
    other_high[...], other_low[...] = split(whole(left[...]))

    def keep_precond(part, values):
        precond[:, :, part] = values.reshape(n, rows, width // 2)

    product_full(other_high, other_low, high, low, keep_precond)
    prec_sum = total(jnp.sum(precond[...] * precond[...], axis=0))
    upper = lax.broadcasted_iota(jnp.int32, norm.shape, 0) < 4
    norm[...] = jnp.where(upper, grad_sum, prec_sum)

    def share(source, target, which, device):
        pltpu.make_async_remote_copy(
            src_ref=source,
            dst_ref=target,
            send_sem=norm_send.at[which],
            recv_sem=norm_recv.at[which],
            device_id=device,
            device_id_type=MESH,
        ).start()

    def share_pre(k, _):
        share(norm_group, norm_pre.at[group], 1, {"pre": (group + k) % groups})
        return 0

    def share_train(k, _):
        share(norm_all, norm_all, 2, {"train": k})
        return 0

    @pl.when(me != 0)
    def _():
        share(norm, norm_train.at[me], 0, {"train": 0})

    send_root(left, left_in, 2)

    @pl.when(me == 0)
    def _():
        norm_train[0] = norm[...]
        wait_bytes(norm_train, norm_recv.at[0])
        norm_group[...] = jnp.sum(norm_train[...], axis=0)
        lax.fori_loop(1, groups, share_pre, 0)
        norm_pre[group] = norm_group[...]

    wait_bytes(right_in, recv_sems.at[1], root_chunks)
    exchange(right_in, 0)
    send_part(precond, precond_in, 3, 0, n * 11 // 16)

    @pl.when(me == 0)
    def _():
        wait_bytes(norm_pre, norm_recv.at[1], groups - 1)
        wait_bytes(norm_pre, norm_send.at[1], groups - 1)
        norm_all[...] = jnp.sum(norm_pre[...], axis=0)
        lax.fori_loop(1, n, share_train, 0)

    wait_bytes(left_in, recv_sems.at[2], root_chunks)
    exchange(left_in, 1)
    send_part(precond, precond_in, 3, n * 11 // 16, n - 1)
    keep_own = pltpu.make_async_copy(precond.at[me], precond_in.at[me], out_sems.at[4])
    keep_own.start()

    def to_blocks(source, target, which):
        def move(block, _):
            ready[which, block] = source[place[block]]
            return 0

        lax.fori_loop(0, blocks, move, 0)
        store = pltpu.make_async_copy(ready.at[which], target, out_sems.at[2 + which])
        store.start()
        return store

    place_crossed(right_in, 0)
    store_right = to_blocks(right_in, right_root_hbm, 1)
    place_crossed(left_in, 1)
    store_left = to_blocks(left_in, left_root_hbm, 0)

    @pl.when(me != 0)
    def _():
        pltpu.make_async_copy(norm, norm, norm_send.at[0]).wait()
        pltpu.make_async_copy(norm_all, norm_all, norm_recv.at[2]).wait()

    @pl.when(me == 0)
    def _():
        wait_bytes(norm_train, norm_send.at[2])

    store_norm = pltpu.make_async_copy(norm_all, norm_hbm, out_sems.at[5])
    store_norm.start()
    wait_bytes(owned, send_sems.at[0])
    wait_bytes(right, send_sems.at[1], root_chunks)
    wait_bytes(left, send_sems.at[2], root_chunks)
    for which in range(2):
        pltpu.make_async_copy(turned.at[which], turned.at[which], cross_send.at[which]).wait()
    wait_bytes(precond, send_sems.at[3])
    store_left_stat.wait()
    store_right_stat.wait()
    store_left.wait()
    store_right.wait()
    store_norm.wait()
    keep_own.wait()
    wait_bytes(precond_in, recv_sems.at[3])


def in_hbm(value):
    return pltpu.with_memory_space_constraint(value, pltpu.HBM)


def copy_in_parts(source, target, sems):
    count = source.shape[0] // 4
    parts = [pl.ds(part * count, count) for part in range(4)]
    copies = [
        pltpu.make_async_copy(source.at[at], target.at[at], sems.at[part])
        for part, at in enumerate(parts)
    ]
    for copy in copies:
        copy.start()
    return copies


def deliver(
    order_hbm, precond_hbm, left, right, left_stat, right_stat, norm_hbm,
    update, left_out, right_out, left_stat_out, right_stat_out,
    precond, norm, order, in_sems, out_sems,
):
    blocks = precond.shape[0]
    load_order = pltpu.make_async_copy(order_hbm, order, in_sems.at[4])
    load_norm = pltpu.make_async_copy(norm_hbm, norm, in_sems.at[5])
    load_order.start()
    load_norm.start()
    loads = copy_in_parts(precond_hbm, precond, in_sems)
    pairs = ((left, left_out), (right, right_out), (left_stat, left_stat_out), (right_stat, right_stat_out))
    stores = []
    for i, (source, target) in enumerate(pairs):
        stores += copy_in_parts(source, target, out_sems.at[pl.ds(4 * i, 4)])
    load_order.wait()
    load_norm.wait()
    graft = jnp.sqrt(norm[0:1, 0:1] / (norm[4:5, 0:1] + 1e-6))

    def scale(slot, _):
        precond[slot] = precond[slot] * graft
        pltpu.make_async_copy(
            precond.at[slot], update.at[order[0, slot]], out_sems.at[16]
        ).start()
        return 0

    for part, load in enumerate(loads):
        load.wait()
        lax.fori_loop(part * (blocks // 4), (part + 1) * (blocks // 4), scale, 0)
    for store in stores:
        store.wait()
    pltpu.make_async_copy(precond, update, out_sems.at[16]).wait()


def shards(gradient, assignment, left_prev, right_prev):
    n, groups = lax.axis_size("train"), lax.axis_size("pre")
    blocks, rows, width = gradient.shape
    pieces = jax.ShapeDtypeStruct((blocks, rows, width), jnp.float32)
    square = jax.ShapeDtypeStruct((width, width), jnp.float32)
    any_space = pl.BlockSpec(memory_space=pl.ANY)
    pieces_vmem = pltpu.VMEM(pieces.shape, jnp.float32)
    square_vmem = pltpu.VMEM(square.shape, jnp.float32)
    square_half = pltpu.VMEM(square.shape, jnp.bfloat16)
    results = (pieces, pieces, pieces, square, square)
    made = pl.pallas_call(
        body,
        out_shape=results + (jax.ShapeDtypeStruct((8, 128), jnp.float32),),
        in_specs=[pl.BlockSpec(memory_space=pltpu.HBM)] * 4,
        out_specs=(any_space,) * 6,
        scratch_shapes=[pieces_vmem] * 3
        + [square_vmem] * 4
        + [pieces_vmem] * 5
        + [
            pltpu.VMEM((2,) + pieces.shape, jnp.float32),
            pltpu.VMEM((2, 2, SUBS, rows, width // PAIRS), jnp.float32),
            pltpu.VMEM((2, n // PAIRS, rows, width // PAIRS), jnp.float32),
        ]
        + [square_half] * 4
        + [
            pltpu.VMEM((ITERS,) + square.shape, jnp.bfloat16),
            square_half,
            square_half,
            pltpu.VMEM((ITERS - 1,) + square.shape, jnp.bfloat16),
            pltpu.VMEM((ITERS - 1,) + square.shape, jnp.bfloat16),
            pltpu.VMEM((8, 128), jnp.float32),
            pltpu.VMEM((8, 128), jnp.float32),
            pltpu.VMEM((8, 128), jnp.float32),
            pltpu.VMEM((groups, 8, 128), jnp.float32),
            pltpu.VMEM((n, 8, 128), jnp.float32),
            pltpu.SMEM((1, blocks), jnp.int32),
            pltpu.SMEM((blocks,), jnp.int32),
            pltpu.SemaphoreType.DMA((8,)),
            pltpu.SemaphoreType.DMA((6,)),
            pltpu.SemaphoreType.DMA((4,)),
            pltpu.SemaphoreType.DMA((2,)),
            pltpu.SemaphoreType.DMA((4,)),
            pltpu.SemaphoreType.DMA((2,)),
            pltpu.SemaphoreType.DMA((2,)),
            pltpu.SemaphoreType.DMA((3,)),
            pltpu.SemaphoreType.DMA((3,)),
        ],
        compiler_params=pltpu.CompilerParams(
            collective_id=0, has_side_effects=True, vmem_limit_bytes=48 * 2**20
        ),
        cost_estimate=pl.CostEstimate(
            flops=2 * 28 * width**3, bytes_accessed=32 * width**2, transcendentals=0
        ),
        name="shampoo",
    )(*(in_hbm(value) for value in (assignment, gradient, left_prev[0, 0], right_prev[0, 0])))
    update, left_root, right_root, left_stat, right_stat = pl.pallas_call(
        deliver,
        out_shape=results,
        in_specs=[any_space] * 7,
        out_specs=(pl.BlockSpec(memory_space=pltpu.HBM),) * 5,
        scratch_shapes=[
            pieces_vmem,
            pltpu.VMEM((8, 128), jnp.float32),
            pltpu.SMEM((1, blocks), jnp.int32),
            pltpu.SemaphoreType.DMA((6,)),
            pltpu.SemaphoreType.DMA((17,)),
        ],
        compiler_params=pltpu.CompilerParams(vmem_limit_bytes=4 * 2**20),
        name="deliver",
    )(in_hbm(assignment), *made)
    return update, left_root, right_root, left_stat[None, None], right_stat[None, None]


def solution(mesh):
    by_rows = P("pre", "train", None)
    by_owner = P("pre", "train", None, None)
    return jax.shard_map(
        shards,
        mesh=mesh,
        in_specs=(by_rows, P("pre", None), by_owner, by_owner),
        out_specs=(by_rows, by_rows, by_rows, by_owner, by_owner),
        check_vma=False,
    )
```

```python
import functools

import jax
import jax.numpy as jnp
from jax import lax
from jax.experimental import pallas as pl
from jax.experimental.pallas import tpu as pltpu
from jax.sharding import PartitionSpec as P

MESH = pl.DeviceIdType.MESH
DECAY = 0.95
ITERS = 3
RINGS = 8
SUBS = 4
PAIRS = 4


def split(values):
    high = values.astype(jnp.bfloat16)
    low = (values - high.astype(jnp.float32)).astype(jnp.bfloat16)
    return high, low


def dot(left, right):
    return jnp.dot(left, right, preferred_element_type=jnp.float32)


def dot_t(left, right):
    return lax.dot_general(
        left, right, (((1,), (1,)), ((), ())), preferred_element_type=jnp.float32
    )


def total(values):
    return jnp.sum(jnp.sum(values, axis=0, keepdims=True), axis=1, keepdims=True)


def halves(width):
    return [slice(start, start + width // 2) for start in (0, width // 2)]


def product(left, right, finish):
    for part in halves(right.shape[1]):
        finish(part, dot(left[...], right[:, part]))


def product_full(left_high, left_low, right_high, right_low, finish):
    for part in halves(right_high.shape[1]):
        cross = dot(left_high[...], right_low[:, part]) + dot(left_low[...], right_high[:, part])
        finish(part, dot(left_high[...], right_high[:, part]) + cross)


def keep(target):
    def finish(part, values):
        target[:, part] = values.astype(target.dtype)

    return finish


def put_factor(factor, part, iterate):
    for rows in halves(factor.shape[0]):
        values = -0.25 * iterate[rows]
        if rows == part:
            shape = values.shape
            diagonal = lax.broadcasted_iota(jnp.int32, shape, 0) == lax.broadcasted_iota(
                jnp.int32, shape, 1
            )
            values = jnp.where(diagonal, 1.25 + values, values)
        factor[rows, part] = values.astype(jnp.bfloat16)


def inverse_root(stat, squares, factor, square, fourth, iterate, root, finish):
    scale = 2.5 / jnp.sqrt(squares)
    start = jnp.sqrt(jnp.sqrt(scale)).astype(jnp.bfloat16).astype(jnp.float32)
    for part in halves(stat.shape[1]):
        values = scale * stat[:, part]
        iterate[0, :, part] = values.astype(jnp.bfloat16)
        put_factor(factor.at[0], part, values)
        root[0, :, part] = (start * factor[0, :, part].astype(jnp.float32)).astype(jnp.bfloat16)

    def advance(now, last):
        def finish_iterate(part, values):
            if not last:
                iterate[now + 1, :, part] = values.astype(jnp.bfloat16)
            put_factor(factor.at[now + 1], part, values)

        product(factor.at[now], factor.at[now], keep(square))
        product(square, square, keep(fourth))
        product(fourth, iterate.at[now], finish_iterate)

    advance(0, False)
    product(root.at[0], factor.at[1], keep(root.at[1]))
    advance(1, True)
    product(root.at[1], factor.at[2], finish)


def body(
    order_hbm, grad_hbm, left_prev, right_prev,
    precond_in, left_root_hbm, right_root_hbm, left_stat_hbm, right_stat_hbm, norm_hbm,
    grad, outgoing, owned, left_old, right_old, left_new, right_new,
    left, right, precond, left_in, right_in, ready, packed, packed_in, turned, crossed, doubled,
    high, low, other_high, other_low, factor, square, fourth, iterate, root,
    norm, norm_group, norm_all, norm_pre, norm_train, order, place,
    in_sems, out_sems, send_sems, recv_grad, recv_sems,
    cross_send, cross_recv, norm_send, norm_recv,
):
    me, group = lax.axis_index("train"), lax.axis_index("pre")
    n, groups = lax.axis_size("train"), lax.axis_size("pre")
    blocks, rows, width = grad.shape
    plane, y_at, core_at = me // SUBS, (me // 2) % 2, me % 2
    pair, upper_plane, peers = plane // 2, plane % 2, n // PAIRS
    tile = width // PAIRS

    barrier = pltpu.get_barrier_semaphore()

    load_left = pltpu.make_async_copy(left_prev, left_old, in_sems.at[1])
    load_right = pltpu.make_async_copy(right_prev, right_old, in_sems.at[2])
    load_order = pltpu.make_async_copy(order_hbm, order, in_sems.at[3])
    load_order.start()
    load_grad = copy_in_parts(grad_hbm, grad, in_sems.at[pl.ds(4, 4)])
    load_left.start()
    load_right.start()
    def greet_train(k, _):
        pl.semaphore_signal(
            barrier, inc=1, device_id={"train": (me + k) % n}, device_id_type=MESH
        )
        return 0

    def greet_pre(k, _):
        pl.semaphore_signal(
            barrier, inc=1, device_id={"pre": (group + k) % groups}, device_id_type=MESH
        )
        return 0

    lax.fori_loop(1, n, greet_train, 0)

    @pl.when(me == 0)
    def _():
        lax.fori_loop(1, groups, greet_pre, 0)

    load_order.wait()
    for load in load_grad:
        load.wait()

    def pick(slot, _):
        outgoing[slot] = grad[order[0, slot]]
        return 0

    lax.fori_loop(0, n, pick, 0)
    pl.semaphore_wait(barrier, n - 1 + jnp.where(me == 0, groups - 1, 0))

    def away(step, core):
        return (RINGS - step) // 2 * (2 * (step % 2) - 1) * (1 - 2 * core)

    def device_at(dz, sub):
        z = (plane + dz + RINGS) % RINGS
        return (z * 2 + (y_at + sub // 2) % 2) * 2 + (core_at + sub) % 2

    def push(source, target, send_sem, recv_sem, other):
        pltpu.make_async_remote_copy(
            src_ref=source,
            dst_ref=target,
            send_sem=send_sem,
            recv_sem=recv_sem,
            device_id={"train": other},
            device_id_type=MESH,
        ).start()

    def send_grad(core, half, step):
        across = (half + step) % 2
        other_core = (core_at + core) % 2
        other = device_at(away(step, core_at), 2 * across + other_core)
        at = half * (n // 2) + 2 * step + 1 - other_core

        @pl.when(other != me)
        def _():
            push(outgoing.at[other], owned.at[at], send_sems.at[0], recv_grad.at[half], other)

    def grad_sender(slot):
        half, step, other_core = slot // (n // 2), slot % (n // 2) // 2, 1 - slot % 2
        dz = away(step, (core_at + other_core) % 2)
        return device_at(-dz, 2 * ((half + step) % 2) + other_core)

    def send_part(source, target, which, first, last):
        def send(k, _):
            step = k % RINGS
            other = device_at(away(step, core_at), (step + k // RINGS + 2) % SUBS)
            push(source.at[other], target.at[me], send_sems.at[which], recv_sems.at[which], other)
            return 0

        lax.fori_loop(first, last, send, 0)

    def columns(which_pair):
        return pl.ds(pl.multiple_of(lax.rem(which_pair, PAIRS) * tile, tile), tile)

    sign = 1 - 2 * upper_plane
    span = SUBS * rows

    def lanes(count, size):
        return lax.broadcasted_iota(jnp.int32, (count, tile), 1) // size

    def send_root(source, target, which):
        send_sem, recv_sem = send_sems.at[which], recv_sems.at[which]
        opposite = (plane + RINGS // 2) % RINGS * SUBS
        for place in range(SUBS):
            ours = source[opposite + place, :, columns(pair)]
            theirs = pltpu.roll(source[opposite + place, :, columns(pair + 2)], span, 1)
            packed[which - 1, place] = jnp.where(lanes(rows, span) == upper_plane, ours, theirs)

        def send(k, _):
            step = k % 6
            dz = (6 - step) // 2 * (1 - 2 * (step % 2)) * sign
            other = device_at(dz, (step + k // 6) % SUBS)
            push(source.at[other], target.at[me], send_sem, recv_sem, other)
            return 0

        def send_packed(place, _):
            mine = me % SUBS
            push(
                packed.at[which - 1, place], packed_in.at[which - 1, mine],
                send_sem, recv_sem, opposite + place,
            )
            return 0

        def send_both(k, _):
            other = (plane - 3 * sign + RINGS) % RINGS * SUBS + k // (PAIRS - 1)
            at = columns(pair + PAIRS + 2 * upper_plane + k % (PAIRS - 1))
            push(source.at[other, :, at], target.at[me, :, at], send_sem, recv_sem, other)
            return send(k, 0)

        tiles = SUBS * (PAIRS - 1)
        lax.fori_loop(0, tiles, send_both, 0)
        lax.fori_loop(0, SUBS, send_packed, 0)
        lax.fori_loop(tiles, n - peers - 1, send, 0)
        target[me] = source[me]

    root_chunks = n - peers - 1 + SUBS

    ring = (3, -3, 2, -2, 1, -1)

    def wrapped(z):
        return lax.rem(z + RINGS, RINGS)

    def exchange(target, which):
        def give(k, to, owners):
            to, owners = wrapped(to), wrapped(owners)
            at = columns(lax.div(to, 2))
            held = target[pl.ds(owners * SUBS, SUBS), :, at].reshape(span, tile)
            doubled[:span], doubled[span:] = held, held
            both = doubled[...].T
            part = jnp.where(lax.rem(to, 2) == 1, both[span:], both[:span])
            part = part.reshape(SUBS, 2, rows // 2, tile)
            first = (lanes(rows // 2, span) == 0)[None]
            turned[which, k] = jnp.where(first, part[:, 0], part[:, 1])

            def send(place, _):
                push(
                    turned.at[which, k, place], crossed.at[which, k, me % SUBS],
                    cross_send.at[which], cross_recv.at[which], to * SUBS + place,
                )
                return 0

            lax.fori_loop(0, SUBS, send, 0)

        for k, dz in enumerate(ring):
            give(k, plane + dz, plane + dz + RINGS // 2)
        give(6, plane + 2 * sign, plane - sign)
        give(7, plane - sign, plane + 2 * sign)

    def place_crossed(target, which):
        arrived = crossed.at[which]
        pltpu.make_async_copy(arrived, arrived, cross_recv.at[which]).wait()
        opposite, beside = wrapped(plane + RINGS // 2), wrapped(plane - 3 * sign)
        missing = columns(pair + 3 + 2 * upper_plane)
        halfway = rows // 2
        mine = lanes(rows, span) == upper_plane
        for block in range(SUBS):
            target[opposite * SUBS + block] = jnp.zeros((rows, width), jnp.float32)
            target[beside * SUBS + block, :, missing] = jnp.zeros((rows, tile), jnp.float32)
            direct = packed_in[which, block]
            for at, values in ((pair + 2, direct), (pair, pltpu.roll(direct, span, 1))):
                target[opposite * SUBS + block, :, columns(at)] = jnp.where(mine, values, 0.0)

        def take(k, giver, owners):
            giver = wrapped(giver)
            at, odd = columns(lax.div(giver, 2)), lax.rem(giver, 2)
            pieces = [crossed[which, k, sender] for sender in range(SUBS)]
            for block in range(SUBS):
                where = owners * SUBS + block
                top, bottom = target[where, :halfway, at], target[where, halfway:, at]
                for sender in range(SUBS):
                    shift = rows * ((sender - block) % (2 * SUBS))
                    near, far = (
                        pltpu.roll(pieces[sender], by, 1) if by else pieces[sender]
                        for by in (shift, (shift + span) % tile)
                    )
                    here = lanes(halfway, rows) == SUBS * odd + sender
                    top = jnp.where(here, jnp.where(odd == 1, far, near), top)
                    bottom = jnp.where(here, jnp.where(odd == 1, near, far), bottom)
                target[where, :halfway, at] = top
                target[where, halfway:, at] = bottom

        for k, dz in enumerate(ring):
            take(k, plane - dz, opposite)
        take(6, plane - 2 * sign, beside)
        take(7, plane - sign, beside)

    def wait_bytes(ref, sem, count=n - 1):
        some = ref.at[pl.ds(0, count)]
        pltpu.make_async_copy(some, some, sem).wait()

    def send_mixed(half, first, k, _):
        for step in range(4):
            send_grad(0, half, 4 * k + step)
        send_grad(1, 0, first + k)
        return 0

    lax.fori_loop(0, 2, functools.partial(send_mixed, 0, 0), 0)
    lax.fori_loop(0, 2, functools.partial(send_mixed, 1, 2), 0)
    for half, first in ((0, 4), (1, 0)):

        def send_rest(step, _):
            send_grad(1, half, step)
            return 0

        lax.fori_loop(first, RINGS, send_rest, 0)
    owned[n - 1] = outgoing[me]

    def invert(block, _):
        def look(slot, found):
            return jnp.where(order[0, slot] == block, slot, found)

        place[block] = lax.fori_loop(0, n, look, 0)
        return 0

    lax.fori_loop(0, blocks, invert, 0)
    grad_sum = total(jnp.sum(grad[...] * grad[...], axis=0))

    def whole(values, count=n):
        return values.reshape(count * rows, width)

    def gram_of(half):
        count = n // 2
        some_high, some_low = split(whole(owned[half * count : (half + 1) * count], count))
        turned_high, turned_low = some_high.T, some_low.T
        for part in halves(width):
            cross = dot(turned_high, some_low[:, part]) + dot(turned_low, some_high[:, part])
            yield part, dot(turned_high, some_high[:, part]) + cross

    def keep_stat(stat, parts):
        squares = jnp.zeros((1, width // 2), jnp.float32)
        for part, values in parts:
            stat[:, part] = values
            squares += jnp.sum(values * values, axis=0, keepdims=True)
        return jnp.sum(squares, axis=1, keepdims=True)

    def put_root(stat, squares, target):
        def finish(part, values):
            target[:, :, part] = values.reshape(n, rows, width // 2)

        inverse_root(stat, squares, factor, square, fourth, iterate, root, finish)

    load_right.wait()
    wait_bytes(owned, recv_grad.at[0], n // 2)
    for part, gram in gram_of(0):
        right_new[:, part] = DECAY * right_old[:, part] + (1.0 - DECAY) * gram
    wait_bytes(owned.at[pl.ds(n // 2, n // 2)], recv_grad.at[1], n // 2 - 1)
    squares = keep_stat(
        right_new,
        [
            (part, right_new[:, part] + (1.0 - DECAY) * gram)
            for part, gram in gram_of(1)
        ],
    )
    store_right_stat = pltpu.make_async_copy(right_new, right_stat_hbm, out_sems.at[1])
    store_right_stat.start()
    put_root(right_new, squares, right)
    send_root(right, right_in, 1)

    def place_rows(k, _):
        at = pl.ds(pl.multiple_of(grad_sender(k) * rows, rows), rows)
        high[at], low[at] = split(owned[k])
        return 0

    lax.fori_loop(0, n, place_rows, 0)
    load_left.wait()
    parts = []
    for part in halves(width):
        gram = dot_t(high[...], high[part]) + (
            dot_t(high[...], low[part]) + dot_t(low[...], high[part])
        )
        parts.append((part, DECAY * left_old[:, part] + (1.0 - DECAY) * gram))
    squares = keep_stat(left_new, parts)
    store_left_stat = pltpu.make_async_copy(left_new, left_stat_hbm, out_sems.at[0])
    store_left_stat.start()
    put_root(left_new, squares, left)

    def keep_split(part, values):
        right_old[:, part] = values

    other_high[...], other_low[...] = split(whole(right[...]))
    product_full(high, low, other_high, other_low, keep_split)
    high[...], low[...] = split(right_old[...])
    other_high[...], other_low[...] = split(whole(left[...]))

    def keep_precond(part, values):
        precond[:, :, part] = values.reshape(n, rows, width // 2)

    product_full(other_high, other_low, high, low, keep_precond)
    prec_sum = total(jnp.sum(precond[...] * precond[...], axis=0))
    upper = lax.broadcasted_iota(jnp.int32, norm.shape, 0) < 4
    norm[...] = jnp.where(upper, grad_sum, prec_sum)

    def share(source, target, which, device):
        pltpu.make_async_remote_copy(
            src_ref=source,
            dst_ref=target,
            send_sem=norm_send.at[which],
            recv_sem=norm_recv.at[which],
            device_id=device,
            device_id_type=MESH,
        ).start()

    def share_pre(k, _):
        share(norm_group, norm_pre.at[group], 1, {"pre": (group + k) % groups})
        return 0

    def share_train(k, _):
        share(norm_all, norm_all, 2, {"train": k})
        return 0

    @pl.when(me != 0)
    def _():
        share(norm, norm_train.at[me], 0, {"train": 0})

    send_root(left, left_in, 2)

    @pl.when(me == 0)
    def _():
        norm_train[0] = norm[...]
        wait_bytes(norm_train, norm_recv.at[0])
        norm_group[...] = jnp.sum(norm_train[...], axis=0)
        lax.fori_loop(1, groups, share_pre, 0)
        norm_pre[group] = norm_group[...]

    wait_bytes(right_in, recv_sems.at[1], root_chunks)
    exchange(right_in, 0)
    send_part(precond, precond_in, 3, 0, n * 9 // 16)

    @pl.when(me == 0)
    def _():
        wait_bytes(norm_pre, norm_recv.at[1], groups - 1)
        wait_bytes(norm_pre, norm_send.at[1], groups - 1)
        norm_all[...] = jnp.sum(norm_pre[...], axis=0)
        lax.fori_loop(1, n, share_train, 0)

    wait_bytes(left_in, recv_sems.at[2], root_chunks)
    exchange(left_in, 1)
    send_part(precond, precond_in, 3, n * 9 // 16, n - 1)
    keep_own = pltpu.make_async_copy(precond.at[me], precond_in.at[me], out_sems.at[4])
    keep_own.start()

    def to_blocks(source, target, which):
        def move(block, _):
            ready[which, block] = source[place[block]]
            return 0

        lax.fori_loop(0, blocks, move, 0)
        store = pltpu.make_async_copy(ready.at[which], target, out_sems.at[2 + which])
        store.start()
        return store

    place_crossed(right_in, 0)
    store_right = to_blocks(right_in, right_root_hbm, 1)
    place_crossed(left_in, 1)
    store_left = to_blocks(left_in, left_root_hbm, 0)

    @pl.when(me != 0)
    def _():
        pltpu.make_async_copy(norm, norm, norm_send.at[0]).wait()
        pltpu.make_async_copy(norm_all, norm_all, norm_recv.at[2]).wait()

    @pl.when(me == 0)
    def _():
        wait_bytes(norm_train, norm_send.at[2])

    store_norm = pltpu.make_async_copy(norm_all, norm_hbm, out_sems.at[5])
    store_norm.start()
    wait_bytes(owned, send_sems.at[0])
    wait_bytes(right, send_sems.at[1], root_chunks)
    wait_bytes(left, send_sems.at[2], root_chunks)
    for which in range(2):
        pltpu.make_async_copy(turned.at[which], turned.at[which], cross_send.at[which]).wait()
    wait_bytes(precond, send_sems.at[3])
    store_left_stat.wait()
    store_right_stat.wait()
    store_left.wait()
    store_right.wait()
    store_norm.wait()
    keep_own.wait()
    wait_bytes(precond_in, recv_sems.at[3])


def in_hbm(value):
    return pltpu.with_memory_space_constraint(value, pltpu.HBM)


def copy_in_parts(source, target, sems):
    count = source.shape[0] // 4
    parts = [pl.ds(part * count, count) for part in range(4)]
    copies = [
        pltpu.make_async_copy(source.at[at], target.at[at], sems.at[part])
        for part, at in enumerate(parts)
    ]
    for copy in copies:
        copy.start()
    return copies


def deliver(
    order_hbm, precond_hbm, left, right, left_stat, right_stat, norm_hbm,
    update, left_out, right_out, left_stat_out, right_stat_out,
    precond, norm, order, in_sems, out_sems,
):
    blocks = precond.shape[0]
    load_order = pltpu.make_async_copy(order_hbm, order, in_sems.at[4])
    load_norm = pltpu.make_async_copy(norm_hbm, norm, in_sems.at[5])
    load_order.start()
    load_norm.start()
    loads = copy_in_parts(precond_hbm, precond, in_sems)
    pairs = ((left, left_out), (right, right_out), (left_stat, left_stat_out), (right_stat, right_stat_out))
    stores = []
    for i, (source, target) in enumerate(pairs):
        stores += copy_in_parts(source, target, out_sems.at[pl.ds(4 * i, 4)])
    load_order.wait()
    load_norm.wait()
    graft = jnp.sqrt(norm[0:1, 0:1] / (norm[4:5, 0:1] + 1e-6))

    def scale(slot, _):
        precond[slot] = precond[slot] * graft
        pltpu.make_async_copy(
            precond.at[slot], update.at[order[0, slot]], out_sems.at[16]
        ).start()
        return 0

    for part, load in enumerate(loads):
        load.wait()
        lax.fori_loop(part * (blocks // 4), (part + 1) * (blocks // 4), scale, 0)
    for store in stores:
        store.wait()
    pltpu.make_async_copy(precond, update, out_sems.at[16]).wait()


def shards(gradient, assignment, left_prev, right_prev):
    n, groups = lax.axis_size("train"), lax.axis_size("pre")
    blocks, rows, width = gradient.shape
    pieces = jax.ShapeDtypeStruct((blocks, rows, width), jnp.float32)
    square = jax.ShapeDtypeStruct((width, width), jnp.float32)
    any_space = pl.BlockSpec(memory_space=pl.ANY)
    pieces_vmem = pltpu.VMEM(pieces.shape, jnp.float32)
    square_vmem = pltpu.VMEM(square.shape, jnp.float32)
    square_half = pltpu.VMEM(square.shape, jnp.bfloat16)
    results = (pieces, pieces, pieces, square, square)
    made = pl.pallas_call(
        body,
        out_shape=results + (jax.ShapeDtypeStruct((8, 128), jnp.float32),),
        in_specs=[pl.BlockSpec(memory_space=pltpu.HBM)] * 4,
        out_specs=(any_space,) * 6,
        scratch_shapes=[pieces_vmem] * 3
        + [square_vmem] * 4
        + [pieces_vmem] * 5
        + [
            pltpu.VMEM((2,) + pieces.shape, jnp.float32),
            pltpu.VMEM((2, SUBS, rows, width // PAIRS), jnp.float32),
            pltpu.VMEM((2, SUBS, rows, width // PAIRS), jnp.float32),
            pltpu.VMEM((2, 8, SUBS, rows // 2, width // PAIRS), jnp.float32),
            pltpu.VMEM((2, 8, SUBS, rows // 2, width // PAIRS), jnp.float32),
            pltpu.VMEM((width // PAIRS, width // PAIRS), jnp.float32),
        ]
        + [square_half] * 4
        + [
            pltpu.VMEM((ITERS,) + square.shape, jnp.bfloat16),
            square_half,
            square_half,
            pltpu.VMEM((ITERS - 1,) + square.shape, jnp.bfloat16),
            pltpu.VMEM((ITERS - 1,) + square.shape, jnp.bfloat16),
            pltpu.VMEM((8, 128), jnp.float32),
            pltpu.VMEM((8, 128), jnp.float32),
            pltpu.VMEM((8, 128), jnp.float32),
            pltpu.VMEM((groups, 8, 128), jnp.float32),
            pltpu.VMEM((n, 8, 128), jnp.float32),
            pltpu.SMEM((1, blocks), jnp.int32),
            pltpu.SMEM((blocks,), jnp.int32),
            pltpu.SemaphoreType.DMA((8,)),
            pltpu.SemaphoreType.DMA((6,)),
            pltpu.SemaphoreType.DMA((4,)),
            pltpu.SemaphoreType.DMA((2,)),
            pltpu.SemaphoreType.DMA((4,)),
            pltpu.SemaphoreType.DMA((2,)),
            pltpu.SemaphoreType.DMA((2,)),
            pltpu.SemaphoreType.DMA((3,)),
            pltpu.SemaphoreType.DMA((3,)),
        ],
        compiler_params=pltpu.CompilerParams(
            collective_id=0, has_side_effects=True, vmem_limit_bytes=48 * 2**20
        ),
        cost_estimate=pl.CostEstimate(
            flops=2 * 28 * width**3, bytes_accessed=32 * width**2, transcendentals=0
        ),
        name="shampoo",
    )(*(in_hbm(value) for value in (assignment, gradient, left_prev[0, 0], right_prev[0, 0])))
    update, left_root, right_root, left_stat, right_stat = pl.pallas_call(
        deliver,
        out_shape=results,
        in_specs=[any_space] * 7,
        out_specs=(pl.BlockSpec(memory_space=pltpu.HBM),) * 5,
        scratch_shapes=[
            pieces_vmem,
            pltpu.VMEM((8, 128), jnp.float32),
            pltpu.SMEM((1, blocks), jnp.int32),
            pltpu.SemaphoreType.DMA((6,)),
            pltpu.SemaphoreType.DMA((17,)),
        ],
        compiler_params=pltpu.CompilerParams(vmem_limit_bytes=4 * 2**20),
        name="deliver",
    )(in_hbm(assignment), *made)
    return update, left_root, right_root, left_stat[None, None], right_stat[None, None]


def solution(mesh):
    by_rows = P("pre", "train", None)
    by_owner = P("pre", "train", None, None)
    return jax.shard_map(
        shards,
        mesh=mesh,
        in_specs=(by_rows, P("pre", None), by_owner, by_owner),
        out_specs=(by_rows, by_rows, by_rows, by_owner, by_owner),
        check_vma=False,
    )
```

```python
import functools

import jax
import jax.numpy as jnp
from jax import lax
from jax.experimental import pallas as pl
from jax.experimental.pallas import tpu as pltpu
from jax.sharding import PartitionSpec as P

MESH = pl.DeviceIdType.MESH
DECAY = 0.95
ITERS = 3
RINGS = 8
SUBS = 4
PAIRS = 4


def split(values):
    high = values.astype(jnp.bfloat16)
    low = (values - high.astype(jnp.float32)).astype(jnp.bfloat16)
    return high, low


def dot(left, right):
    return jnp.dot(left, right, preferred_element_type=jnp.float32)


def dot_t(left, right):
    return lax.dot_general(
        left, right, (((1,), (1,)), ((), ())), preferred_element_type=jnp.float32
    )


def total(values):
    return jnp.sum(jnp.sum(values, axis=0, keepdims=True), axis=1, keepdims=True)


def halves(width):
    return [slice(start, start + width // 2) for start in (0, width // 2)]


def product(left, right, finish):
    for part in halves(right.shape[1]):
        finish(part, dot(left[...], right[:, part]))


def product_full(left_high, left_low, right_high, right_low, finish):
    for part in halves(right_high.shape[1]):
        cross = dot(left_high[...], right_low[:, part]) + dot(left_low[...], right_high[:, part])
        finish(part, dot(left_high[...], right_high[:, part]) + cross)


def keep(target):
    def finish(part, values):
        target[:, part] = values.astype(target.dtype)

    return finish


def put_factor(factor, part, iterate):
    for rows in halves(factor.shape[0]):
        values = -0.25 * iterate[rows]
        if rows == part:
            shape = values.shape
            diagonal = lax.broadcasted_iota(jnp.int32, shape, 0) == lax.broadcasted_iota(
                jnp.int32, shape, 1
            )
            values = jnp.where(diagonal, 1.25 + values, values)
        factor[rows, part] = values.astype(jnp.bfloat16)


def inverse_root(stat, squares, factor, square, fourth, iterate, root, finish):
    scale = 2.5 / jnp.sqrt(squares)
    start = jnp.sqrt(jnp.sqrt(scale)).astype(jnp.bfloat16).astype(jnp.float32)
    for part in halves(stat.shape[1]):
        values = scale * stat[:, part]
        iterate[0, :, part] = values.astype(jnp.bfloat16)
        put_factor(factor.at[0], part, values)
        root[0, :, part] = (start * factor[0, :, part].astype(jnp.float32)).astype(jnp.bfloat16)

    def advance(now, last):
        def finish_iterate(part, values):
            if not last:
                iterate[now + 1, :, part] = values.astype(jnp.bfloat16)
            put_factor(factor.at[now + 1], part, values)

        product(factor.at[now], factor.at[now], keep(square))
        product(square, square, keep(fourth))
        product(fourth, iterate.at[now], finish_iterate)

    advance(0, False)
    product(root.at[0], factor.at[1], keep(root.at[1]))
    advance(1, True)
    product(root.at[1], factor.at[2], finish)


def body(
    order_hbm, grad_hbm, left_prev, right_prev,
    precond_in, left_root_hbm, right_root_hbm, left_stat_hbm, right_stat_hbm, norm_hbm,
    grad, outgoing, owned, left_old, right_old, left_new, right_new,
    left, right, precond, left_in, right_in, ready, packed, packed_in, turned, crossed, doubled,
    high, low, other_high, other_low, factor, square, fourth, iterate, root,
    norm, norm_group, norm_all, norm_pre, norm_train, order, place,
    in_sems, out_sems, send_sems, recv_grad, recv_sems,
    cross_send, cross_recv, norm_send, norm_recv,
):
    me, group = lax.axis_index("train"), lax.axis_index("pre")
    n, groups = lax.axis_size("train"), lax.axis_size("pre")
    blocks, rows, width = grad.shape
    plane, y_at, core_at = me // SUBS, (me // 2) % 2, me % 2
    pair, upper_plane, peers = plane // 2, plane % 2, n // PAIRS
    tile = width // PAIRS

    barrier = pltpu.get_barrier_semaphore()

    load_left = pltpu.make_async_copy(left_prev, left_old, in_sems.at[1])
    load_right = pltpu.make_async_copy(right_prev, right_old, in_sems.at[2])
    load_order = pltpu.make_async_copy(order_hbm, order, in_sems.at[3])
    load_order.start()
    load_grad = copy_in_parts(grad_hbm, grad, in_sems.at[pl.ds(4, 4)])
    load_left.start()
    load_right.start()
    def greet_train(k, _):
        pl.semaphore_signal(
            barrier, inc=1, device_id={"train": (me + k) % n}, device_id_type=MESH
        )
        return 0

    def greet_pre(k, _):
        pl.semaphore_signal(
            barrier, inc=1, device_id={"pre": (group + k) % groups}, device_id_type=MESH
        )
        return 0

    lax.fori_loop(1, n, greet_train, 0)

    @pl.when(me == 0)
    def _():
        lax.fori_loop(1, groups, greet_pre, 0)

    load_order.wait()
    for load in load_grad:
        load.wait()

    def pick(slot, _):
        outgoing[slot] = grad[order[0, slot]]
        return 0

    lax.fori_loop(0, n, pick, 0)
    pl.semaphore_wait(barrier, n - 1 + jnp.where(me == 0, groups - 1, 0))

    def away(step, core):
        return (RINGS - step) // 2 * (2 * (step % 2) - 1) * (1 - 2 * core)

    def device_at(dz, sub):
        z = (plane + dz + RINGS) % RINGS
        return (z * 2 + (y_at + sub // 2) % 2) * 2 + (core_at + sub) % 2

    def push(source, target, send_sem, recv_sem, other):
        pltpu.make_async_remote_copy(
            src_ref=source,
            dst_ref=target,
            send_sem=send_sem,
            recv_sem=recv_sem,
            device_id={"train": other},
            device_id_type=MESH,
        ).start()

    def send_grad(core, half, step):
        across = (half + step) % 2
        other_core = (core_at + core) % 2
        other = device_at(away(step, core_at), 2 * across + other_core)
        at = half * (n // 2) + 2 * step + 1 - other_core

        @pl.when(other != me)
        def _():
            push(outgoing.at[other], owned.at[at], send_sems.at[0], recv_grad.at[half], other)

    def grad_sender(slot):
        half, step, other_core = slot // (n // 2), slot % (n // 2) // 2, 1 - slot % 2
        dz = away(step, (core_at + other_core) % 2)
        return device_at(-dz, 2 * ((half + step) % 2) + other_core)

    def send_part(source, target, which, first, last):
        def send(k, _):
            step = k % RINGS
            other = device_at(away(step, core_at), (step + k // RINGS + 2) % SUBS)
            push(source.at[other], target.at[me], send_sems.at[which], recv_sems.at[which], other)
            return 0

        lax.fori_loop(first, last, send, 0)

    def columns(which_pair):
        return pl.ds(pl.multiple_of(lax.rem(which_pair, PAIRS) * tile, tile), tile)

    sign = 1 - 2 * upper_plane
    span = SUBS * rows

    def lanes(count, size):
        return lax.broadcasted_iota(jnp.int32, (count, tile), 1) // size

    def send_root(source, target, which):
        send_sem, recv_sem = send_sems.at[which], recv_sems.at[which]
        opposite = (plane + RINGS // 2) % RINGS * SUBS
        across = (plane + 3 * sign + RINGS) % RINGS * SUBS
        next_pair = pair + PAIRS + sign
        for place in range(SUBS):
            ours = source[across + place, :, columns(pair)]
            theirs = source[across + place, :, columns(next_pair)]
            packed[which - 1, SUBS + place] = jnp.where(
                lanes(rows, span) == upper_plane, ours, theirs
            )
            ours = source[opposite + place, :, columns(pair)]
            theirs = pltpu.roll(source[opposite + place, :, columns(pair + 2)], span, 1)
            packed[which - 1, place] = jnp.where(lanes(rows, span) == upper_plane, ours, theirs)

        def send(k, _):
            step = k % 5
            dz = (5 - step) // 2 * (1 - 2 * (step % 2)) * sign
            other = device_at(dz, (step + k // 5 + 1) % SUBS)
            push(source.at[other], target.at[me], send_sem, recv_sem, other)
            return 0

        def send_packed(place, _):
            for kind, first in ((0, opposite), (SUBS, across)):
                push(
                    packed.at[which - 1, kind + place], packed_in.at[which - 1, kind + me % SUBS],
                    send_sem, recv_sem, first + place,
                )
            return 0

        def send_tile(other, at):
            push(source.at[other, :, at], target.at[me, :, at], send_sem, recv_sem, other)

        def send_three(k, _):
            other = (plane - 3 * sign + RINGS) % RINGS * SUBS + k // (PAIRS - 1)
            send_tile(other, columns(pair + PAIRS + 2 * upper_plane + k % (PAIRS - 1)))
            return send(k, 0)

        def send_two(k, _):
            for at in (pair + 2, next_pair + 2):
                send_tile(across + k, columns(at))
            return send(three + k, 0)

        three = SUBS * (PAIRS - 1)
        lax.fori_loop(0, SUBS, send_packed, 0)
        lax.fori_loop(0, three, send_three, 0)
        lax.fori_loop(0, SUBS, send_two, 0)
        lax.fori_loop(three + SUBS, n - three - 1, send, 0)
        target[me] = source[me]

    root_chunks = n - 3 * SUBS - 1 + 7 * SUBS // PAIRS

    ring = (3, -3, 2, -2, 1, -1)

    def wrapped(z):
        return lax.rem(z + RINGS, RINGS)

    def exchange(target, which):
        def give(k, to, owners):
            to, owners = wrapped(to), wrapped(owners)
            at = columns(lax.div(to, 2))
            held = target[pl.ds(owners * SUBS, SUBS), :, at].reshape(span, tile)
            doubled[:span], doubled[span:] = held, held
            both = doubled[...].T
            part = jnp.where(lax.rem(to, 2) == 1, both[span:], both[:span])
            part = part.reshape(SUBS, 2, rows // 2, tile)
            first = (lanes(rows // 2, span) == 0)[None]
            turned[which, k] = jnp.where(first, part[:, 0], part[:, 1])

            def send(place, _):
                push(
                    turned.at[which, k, place], crossed.at[which, k, me % SUBS],
                    cross_send.at[which], cross_recv.at[which], to * SUBS + place,
                )
                return 0

            lax.fori_loop(0, SUBS, send, 0)

        for k, dz in enumerate(ring):
            give(k, plane + dz, plane + dz + RINGS // 2)
        give(6, plane + 2 * sign, plane - sign)
        give(7, plane - sign, plane + 2 * sign)
        give(8, plane - 2 * sign, plane + sign)
        give(9, plane + sign, plane - 2 * sign)

    def place_crossed(target, which):
        arrived = crossed.at[which]
        pltpu.make_async_copy(arrived, arrived, cross_recv.at[which]).wait()
        opposite, beside = wrapped(plane + RINGS // 2), wrapped(plane - 3 * sign)
        across = wrapped(plane + 3 * sign)
        missing = columns(pair + 3 + 2 * upper_plane)
        halfway = rows // 2
        mine = lanes(rows, span) == upper_plane
        for block in range(SUBS):
            target[opposite * SUBS + block] = jnp.zeros((rows, width), jnp.float32)
            target[beside * SUBS + block, :, missing] = jnp.zeros((rows, tile), jnp.float32)
            direct = packed_in[which, block]
            for at, values in ((pair + 2, direct), (pair, pltpu.roll(direct, span, 1))):
                target[opposite * SUBS + block, :, columns(at)] = jnp.where(mine, values, 0.0)
            direct = packed_in[which, SUBS + block]
            where = across * SUBS + block
            target[where, :, columns(pair)] = jnp.where(mine, direct, 0.0)
            target[where, :, columns(pair + PAIRS + sign)] = jnp.where(mine, 0.0, direct)

        def take(k, giver, owners):
            giver = wrapped(giver)
            at, odd = columns(lax.div(giver, 2)), lax.rem(giver, 2)
            pieces = [crossed[which, k, sender] for sender in range(SUBS)]
            for block in range(SUBS):
                where = owners * SUBS + block
                top, bottom = target[where, :halfway, at], target[where, halfway:, at]
                for sender in range(SUBS):
                    shift = rows * ((sender - block) % (2 * SUBS))
                    near, far = (
                        pltpu.roll(pieces[sender], by, 1) if by else pieces[sender]
                        for by in (shift, (shift + span) % tile)
                    )
                    here = lanes(halfway, rows) == SUBS * odd + sender
                    top = jnp.where(here, jnp.where(odd == 1, far, near), top)
                    bottom = jnp.where(here, jnp.where(odd == 1, near, far), bottom)
                target[where, :halfway, at] = top
                target[where, halfway:, at] = bottom

        for k, dz in enumerate(ring):
            take(k, plane - dz, opposite)
        take(6, plane - 2 * sign, beside)
        take(7, plane - sign, beside)
        take(8, plane + 2 * sign, across)
        take(9, plane + sign, across)

    def wait_bytes(ref, sem, count=n - 1):
        some = ref.at[pl.ds(0, count)]
        pltpu.make_async_copy(some, some, sem).wait()

    def send_mixed(half, first, k, _):
        for step in range(4):
            send_grad(0, half, 4 * k + step)
        send_grad(1, 0, first + k)
        return 0

    lax.fori_loop(0, 2, functools.partial(send_mixed, 0, 0), 0)
    lax.fori_loop(0, 2, functools.partial(send_mixed, 1, 2), 0)
    for half, first in ((0, 4), (1, 0)):

        def send_rest(step, _):
            send_grad(1, half, step)
            return 0

        lax.fori_loop(first, RINGS, send_rest, 0)
    owned[n - 1] = outgoing[me]

    def invert(block, _):
        def look(slot, found):
            return jnp.where(order[0, slot] == block, slot, found)

        place[block] = lax.fori_loop(0, n, look, 0)
        return 0

    lax.fori_loop(0, blocks, invert, 0)
    grad_sum = total(jnp.sum(grad[...] * grad[...], axis=0))

    def whole(values, count=n):
        return values.reshape(count * rows, width)

    def gram_of(half):
        count = n // 2
        some_high, some_low = split(whole(owned[half * count : (half + 1) * count], count))
        turned_high, turned_low = some_high.T, some_low.T
        for part in halves(width):
            cross = dot(turned_high, some_low[:, part]) + dot(turned_low, some_high[:, part])
            yield part, dot(turned_high, some_high[:, part]) + cross

    def keep_stat(stat, parts):
        squares = jnp.zeros((1, width // 2), jnp.float32)
        for part, values in parts:
            stat[:, part] = values
            squares += jnp.sum(values * values, axis=0, keepdims=True)
        return jnp.sum(squares, axis=1, keepdims=True)

    def put_root(stat, squares, target):
        def finish(part, values):
            target[:, :, part] = values.reshape(n, rows, width // 2)

        inverse_root(stat, squares, factor, square, fourth, iterate, root, finish)

    load_right.wait()
    wait_bytes(owned, recv_grad.at[0], n // 2)
    for part, gram in gram_of(0):
        right_new[:, part] = DECAY * right_old[:, part] + (1.0 - DECAY) * gram
    wait_bytes(owned.at[pl.ds(n // 2, n // 2)], recv_grad.at[1], n // 2 - 1)
    squares = keep_stat(
        right_new,
        [
            (part, right_new[:, part] + (1.0 - DECAY) * gram)
            for part, gram in gram_of(1)
        ],
    )
    store_right_stat = pltpu.make_async_copy(right_new, right_stat_hbm, out_sems.at[1])
    store_right_stat.start()
    put_root(right_new, squares, right)
    send_root(right, right_in, 1)

    def place_rows(k, _):
        at = pl.ds(pl.multiple_of(grad_sender(k) * rows, rows), rows)
        high[at], low[at] = split(owned[k])
        return 0

    lax.fori_loop(0, n, place_rows, 0)
    load_left.wait()
    parts = []
    for part in halves(width):
        gram = dot_t(high[...], high[part]) + (
            dot_t(high[...], low[part]) + dot_t(low[...], high[part])
        )
        parts.append((part, DECAY * left_old[:, part] + (1.0 - DECAY) * gram))
    squares = keep_stat(left_new, parts)
    store_left_stat = pltpu.make_async_copy(left_new, left_stat_hbm, out_sems.at[0])
    store_left_stat.start()
    put_root(left_new, squares, left)

    def keep_split(part, values):
        right_old[:, part] = values

    other_high[...], other_low[...] = split(whole(right[...]))
    product_full(high, low, other_high, other_low, keep_split)
    high[...], low[...] = split(right_old[...])
    other_high[...], other_low[...] = split(whole(left[...]))

    def keep_precond(part, values):
        precond[:, :, part] = values.reshape(n, rows, width // 2)

    product_full(other_high, other_low, high, low, keep_precond)
    prec_sum = total(jnp.sum(precond[...] * precond[...], axis=0))
    upper = lax.broadcasted_iota(jnp.int32, norm.shape, 0) < 4
    norm[...] = jnp.where(upper, grad_sum, prec_sum)

    def share(source, target, which, device):
        pltpu.make_async_remote_copy(
            src_ref=source,
            dst_ref=target,
            send_sem=norm_send.at[which],
            recv_sem=norm_recv.at[which],
            device_id=device,
            device_id_type=MESH,
        ).start()

    def share_pre(k, _):
        share(norm_group, norm_pre.at[group], 1, {"pre": (group + k) % groups})
        return 0

    def share_train(k, _):
        share(norm_all, norm_all, 2, {"train": k})
        return 0

    @pl.when(me != 0)
    def _():
        share(norm, norm_train.at[me], 0, {"train": 0})

    send_root(left, left_in, 2)

    @pl.when(me == 0)
    def _():
        norm_train[0] = norm[...]
        wait_bytes(norm_train, norm_recv.at[0])
        norm_group[...] = jnp.sum(norm_train[...], axis=0)
        lax.fori_loop(1, groups, share_pre, 0)
        norm_pre[group] = norm_group[...]

    wait_bytes(right_in, recv_sems.at[1], root_chunks)
    exchange(right_in, 0)
    send_part(precond, precond_in, 3, 0, n * 9 // 16)

    @pl.when(me == 0)
    def _():
        wait_bytes(norm_pre, norm_recv.at[1], groups - 1)
        wait_bytes(norm_pre, norm_send.at[1], groups - 1)
        norm_all[...] = jnp.sum(norm_pre[...], axis=0)
        lax.fori_loop(1, n, share_train, 0)

    wait_bytes(left_in, recv_sems.at[2], root_chunks)
    exchange(left_in, 1)
    send_part(precond, precond_in, 3, n * 9 // 16, n - 1)
    keep_own = pltpu.make_async_copy(precond.at[me], precond_in.at[me], out_sems.at[4])
    keep_own.start()

    def to_blocks(source, target, which):
        def move(block, _):
            ready[which, block] = source[place[block]]
            return 0

        lax.fori_loop(0, blocks, move, 0)
        store = pltpu.make_async_copy(ready.at[which], target, out_sems.at[2 + which])
        store.start()
        return store

    place_crossed(right_in, 0)
    store_right = to_blocks(right_in, right_root_hbm, 1)
    place_crossed(left_in, 1)
    store_left = to_blocks(left_in, left_root_hbm, 0)

    @pl.when(me != 0)
    def _():
        pltpu.make_async_copy(norm, norm, norm_send.at[0]).wait()
        pltpu.make_async_copy(norm_all, norm_all, norm_recv.at[2]).wait()

    @pl.when(me == 0)
    def _():
        wait_bytes(norm_train, norm_send.at[2])

    store_norm = pltpu.make_async_copy(norm_all, norm_hbm, out_sems.at[5])
    store_norm.start()
    wait_bytes(owned, send_sems.at[0])
    wait_bytes(right, send_sems.at[1], root_chunks)
    wait_bytes(left, send_sems.at[2], root_chunks)
    for which in range(2):
        pltpu.make_async_copy(turned.at[which], turned.at[which], cross_send.at[which]).wait()
    wait_bytes(precond, send_sems.at[3])
    store_left_stat.wait()
    store_right_stat.wait()
    store_left.wait()
    store_right.wait()
    store_norm.wait()
    keep_own.wait()
    wait_bytes(precond_in, recv_sems.at[3])


def in_hbm(value):
    return pltpu.with_memory_space_constraint(value, pltpu.HBM)


def copy_in_parts(source, target, sems):
    count = source.shape[0] // 4
    parts = [pl.ds(part * count, count) for part in range(4)]
    copies = [
        pltpu.make_async_copy(source.at[at], target.at[at], sems.at[part])
        for part, at in enumerate(parts)
    ]
    for copy in copies:
        copy.start()
    return copies


def deliver(
    order_hbm, precond_hbm, left, right, left_stat, right_stat, norm_hbm,
    update, left_out, right_out, left_stat_out, right_stat_out,
    precond, norm, order, in_sems, out_sems,
):
    blocks = precond.shape[0]
    load_order = pltpu.make_async_copy(order_hbm, order, in_sems.at[4])
    load_norm = pltpu.make_async_copy(norm_hbm, norm, in_sems.at[5])
    load_order.start()
    load_norm.start()
    loads = copy_in_parts(precond_hbm, precond, in_sems)
    pairs = ((left, left_out), (right, right_out), (left_stat, left_stat_out), (right_stat, right_stat_out))
    stores = []
    for i, (source, target) in enumerate(pairs):
        stores += copy_in_parts(source, target, out_sems.at[pl.ds(4 * i, 4)])
    load_order.wait()
    load_norm.wait()
    graft = jnp.sqrt(norm[0:1, 0:1] / (norm[4:5, 0:1] + 1e-6))

    def scale(slot, _):
        precond[slot] = precond[slot] * graft
        pltpu.make_async_copy(
            precond.at[slot], update.at[order[0, slot]], out_sems.at[16]
        ).start()
        return 0

    for part, load in enumerate(loads):
        load.wait()
        lax.fori_loop(part * (blocks // 4), (part + 1) * (blocks // 4), scale, 0)
    for store in stores:
        store.wait()
    pltpu.make_async_copy(precond, update, out_sems.at[16]).wait()


def shards(gradient, assignment, left_prev, right_prev):
    n, groups = lax.axis_size("train"), lax.axis_size("pre")
    blocks, rows, width = gradient.shape
    pieces = jax.ShapeDtypeStruct((blocks, rows, width), jnp.float32)
    square = jax.ShapeDtypeStruct((width, width), jnp.float32)
    any_space = pl.BlockSpec(memory_space=pl.ANY)
    pieces_vmem = pltpu.VMEM(pieces.shape, jnp.float32)
    square_vmem = pltpu.VMEM(square.shape, jnp.float32)
    square_half = pltpu.VMEM(square.shape, jnp.bfloat16)
    results = (pieces, pieces, pieces, square, square)
    made = pl.pallas_call(
        body,
        out_shape=results + (jax.ShapeDtypeStruct((8, 128), jnp.float32),),
        in_specs=[pl.BlockSpec(memory_space=pltpu.HBM)] * 4,
        out_specs=(any_space,) * 6,
        scratch_shapes=[pieces_vmem] * 3
        + [square_vmem] * 4
        + [pieces_vmem] * 5
        + [
            pltpu.VMEM((2,) + pieces.shape, jnp.float32),
            pltpu.VMEM((2, 2 * SUBS, rows, width // PAIRS), jnp.float32),
            pltpu.VMEM((2, 2 * SUBS, rows, width // PAIRS), jnp.float32),
            pltpu.VMEM((2, 10, SUBS, rows // 2, width // PAIRS), jnp.float32),
            pltpu.VMEM((2, 10, SUBS, rows // 2, width // PAIRS), jnp.float32),
            pltpu.VMEM((width // PAIRS, width // PAIRS), jnp.float32),
        ]
        + [square_half] * 4
        + [
            pltpu.VMEM((ITERS,) + square.shape, jnp.bfloat16),
            square_half,
            square_half,
            pltpu.VMEM((ITERS - 1,) + square.shape, jnp.bfloat16),
            pltpu.VMEM((ITERS - 1,) + square.shape, jnp.bfloat16),
            pltpu.VMEM((8, 128), jnp.float32),
            pltpu.VMEM((8, 128), jnp.float32),
            pltpu.VMEM((8, 128), jnp.float32),
            pltpu.VMEM((groups, 8, 128), jnp.float32),
            pltpu.VMEM((n, 8, 128), jnp.float32),
            pltpu.SMEM((1, blocks), jnp.int32),
            pltpu.SMEM((blocks,), jnp.int32),
            pltpu.SemaphoreType.DMA((8,)),
            pltpu.SemaphoreType.DMA((6,)),
            pltpu.SemaphoreType.DMA((4,)),
            pltpu.SemaphoreType.DMA((2,)),
            pltpu.SemaphoreType.DMA((4,)),
            pltpu.SemaphoreType.DMA((2,)),
            pltpu.SemaphoreType.DMA((2,)),
            pltpu.SemaphoreType.DMA((3,)),
            pltpu.SemaphoreType.DMA((3,)),
        ],
        compiler_params=pltpu.CompilerParams(
            collective_id=0, has_side_effects=True, vmem_limit_bytes=48 * 2**20
        ),
        cost_estimate=pl.CostEstimate(
            flops=2 * 28 * width**3, bytes_accessed=32 * width**2, transcendentals=0
        ),
        name="shampoo",
    )(*(in_hbm(value) for value in (assignment, gradient, left_prev[0, 0], right_prev[0, 0])))
    update, left_root, right_root, left_stat, right_stat = pl.pallas_call(
        deliver,
        out_shape=results,
        in_specs=[any_space] * 7,
        out_specs=(pl.BlockSpec(memory_space=pltpu.HBM),) * 5,
        scratch_shapes=[
            pieces_vmem,
            pltpu.VMEM((8, 128), jnp.float32),
            pltpu.SMEM((1, blocks), jnp.int32),
            pltpu.SemaphoreType.DMA((6,)),
            pltpu.SemaphoreType.DMA((17,)),
        ],
        compiler_params=pltpu.CompilerParams(vmem_limit_bytes=4 * 2**20),
        name="deliver",
    )(in_hbm(assignment), *made)
    return update, left_root, right_root, left_stat[None, None], right_stat[None, None]


def solution(mesh):
    by_rows = P("pre", "train", None)
    by_owner = P("pre", "train", None, None)
    return jax.shard_map(
        shards,
        mesh=mesh,
        in_specs=(by_rows, P("pre", None), by_owner, by_owner),
        out_specs=(by_rows, by_rows, by_rows, by_owner, by_owner),
        check_vma=False,
    )
```

```python
import functools

import jax
import jax.numpy as jnp
from jax import lax
from jax.experimental import pallas as pl
from jax.experimental.pallas import tpu as pltpu
from jax.sharding import PartitionSpec as P

MESH = pl.DeviceIdType.MESH
DECAY = 0.95
ITERS = 3
RINGS = 8
SUBS = 4
PAIRS = 4


def split(values):
    high = values.astype(jnp.bfloat16)
    low = (values - high.astype(jnp.float32)).astype(jnp.bfloat16)
    return high, low


def dot(left, right):
    return jnp.dot(left, right, preferred_element_type=jnp.float32)


def dot_t(left, right):
    return lax.dot_general(
        left, right, (((1,), (1,)), ((), ())), preferred_element_type=jnp.float32
    )


def total(values):
    return jnp.sum(jnp.sum(values, axis=0, keepdims=True), axis=1, keepdims=True)


def halves(width):
    return [slice(start, start + width // 2) for start in (0, width // 2)]


def product(left, right, finish):
    for part in halves(right.shape[1]):
        finish(part, dot(left[...], right[:, part]))


def product_full(left_high, left_low, right_high, right_low, finish):
    for part in halves(right_high.shape[1]):
        cross = dot(left_high[...], right_low[:, part]) + dot(left_low[...], right_high[:, part])
        finish(part, dot(left_high[...], right_high[:, part]) + cross)


def keep(target):
    def finish(part, values):
        target[:, part] = values.astype(target.dtype)

    return finish


def put_factor(factor, part, iterate):
    for rows in halves(factor.shape[0]):
        values = -0.25 * iterate[rows]
        if rows == part:
            shape = values.shape
            diagonal = lax.broadcasted_iota(jnp.int32, shape, 0) == lax.broadcasted_iota(
                jnp.int32, shape, 1
            )
            values = jnp.where(diagonal, 1.25 + values, values)
        factor[rows, part] = values.astype(jnp.bfloat16)


def inverse_root(stat, squares, factor, square, fourth, iterate, root, finish):
    scale = 2.5 / jnp.sqrt(squares)
    start = jnp.sqrt(jnp.sqrt(scale)).astype(jnp.bfloat16).astype(jnp.float32)
    for part in halves(stat.shape[1]):
        values = scale * stat[:, part]
        iterate[0, :, part] = values.astype(jnp.bfloat16)
        put_factor(factor.at[0], part, values)
        root[0, :, part] = (start * factor[0, :, part].astype(jnp.float32)).astype(jnp.bfloat16)

    def advance(now, last):
        def finish_iterate(part, values):
            if not last:
                iterate[now + 1, :, part] = values.astype(jnp.bfloat16)
            put_factor(factor.at[now + 1], part, values)

        product(factor.at[now], factor.at[now], keep(square))
        product(square, square, keep(fourth))
        product(fourth, iterate.at[now], finish_iterate)

    advance(0, False)
    product(root.at[0], factor.at[1], keep(root.at[1]))
    advance(1, True)
    product(root.at[1], factor.at[2], finish)


def body(
    order_hbm, grad_hbm, left_prev, right_prev,
    precond_in, left_root_hbm, right_root_hbm, left_stat_hbm, right_stat_hbm, norm_hbm,
    grad, outgoing, owned, left_old, right_old, left_new, right_new,
    left, right, precond, left_in, right_in, ready, packed, packed_in, turned, crossed, doubled,
    high, low, other_high, other_low, factor, square, fourth, iterate, root,
    norm, norm_group, norm_all, norm_pre, norm_train, order, place,
    in_sems, out_sems, send_sems, recv_grad, recv_sems,
    cross_send, cross_recv, norm_send, norm_recv,
):
    me, group = lax.axis_index("train"), lax.axis_index("pre")
    n, groups = lax.axis_size("train"), lax.axis_size("pre")
    blocks, rows, width = grad.shape
    plane, y_at, core_at = me // SUBS, (me // 2) % 2, me % 2
    pair, upper_plane, peers = plane // 2, plane % 2, n // PAIRS
    tile = width // PAIRS

    barrier = pltpu.get_barrier_semaphore()

    load_left = pltpu.make_async_copy(left_prev, left_old, in_sems.at[1])
    load_right = pltpu.make_async_copy(right_prev, right_old, in_sems.at[2])
    load_order = pltpu.make_async_copy(order_hbm, order, in_sems.at[3])
    load_order.start()
    load_grad = copy_in_parts(grad_hbm, grad, in_sems.at[pl.ds(4, 4)])
    load_left.start()
    load_right.start()
    def greet_train(k, _):
        pl.semaphore_signal(
            barrier, inc=1, device_id={"train": (me + k) % n}, device_id_type=MESH
        )
        return 0

    def greet_pre(k, _):
        pl.semaphore_signal(
            barrier, inc=1, device_id={"pre": (group + k) % groups}, device_id_type=MESH
        )
        return 0

    lax.fori_loop(1, n, greet_train, 0)

    @pl.when(me == 0)
    def _():
        lax.fori_loop(1, groups, greet_pre, 0)

    load_order.wait()
    for load in load_grad:
        load.wait()

    def pick(slot, _):
        outgoing[slot] = grad[order[0, slot]]
        return 0

    lax.fori_loop(0, n, pick, 0)
    pl.semaphore_wait(barrier, n - 1 + jnp.where(me == 0, groups - 1, 0))

    def away(step, core):
        return (RINGS - step) // 2 * (2 * (step % 2) - 1) * (1 - 2 * core)

    def device_at(dz, sub):
        z = (plane + dz + RINGS) % RINGS
        return (z * 2 + (y_at + sub // 2) % 2) * 2 + (core_at + sub) % 2

    def push(source, target, send_sem, recv_sem, other):
        pltpu.make_async_remote_copy(
            src_ref=source,
            dst_ref=target,
            send_sem=send_sem,
            recv_sem=recv_sem,
            device_id={"train": other},
            device_id_type=MESH,
        ).start()

    def send_grad(core, half, step):
        across = (half + step) % 2
        other_core = (core_at + core) % 2
        other = device_at(away(step, core_at), 2 * across + other_core)
        at = half * (n // 2) + 2 * step + 1 - other_core

        @pl.when(other != me)
        def _():
            push(outgoing.at[other], owned.at[at], send_sems.at[0], recv_grad.at[half], other)

    def grad_sender(slot):
        half, step, other_core = slot // (n // 2), slot % (n // 2) // 2, 1 - slot % 2
        dz = away(step, (core_at + other_core) % 2)
        return device_at(-dz, 2 * ((half + step) % 2) + other_core)

    def send_part(source, target, which, first, last):
        def send(k, _):
            step = k % RINGS
            other = device_at(away(step, core_at), (step + k // RINGS + 2) % SUBS)
            push(source.at[other], target.at[me], send_sems.at[which], recv_sems.at[which], other)
            return 0

        lax.fori_loop(first, last, send, 0)

    def columns(which_pair):
        return pl.ds(pl.multiple_of(lax.rem(which_pair, PAIRS) * tile, tile), tile)

    sign = 1 - 2 * upper_plane
    span = SUBS * rows

    def lanes(count, size):
        return lax.broadcasted_iota(jnp.int32, (count, tile), 1) // size

    def send_root(source, target, which):
        send_sem, recv_sem = send_sems.at[which], recv_sems.at[which]
        opposite = (plane + RINGS // 2) % RINGS * SUBS
        across = (plane + 3 * sign + RINGS) % RINGS * SUBS
        next_pair = pair + PAIRS + sign
        for place in range(SUBS):
            ours = source[across + place, :, columns(pair)]
            theirs = source[across + place, :, columns(next_pair)]
            packed[which - 1, SUBS + place] = jnp.where(
                lanes(rows, span) == upper_plane, ours, theirs
            )
            ours = source[opposite + place, :, columns(pair)]
            theirs = pltpu.roll(source[opposite + place, :, columns(pair + 2)], span, 1)
            packed[which - 1, place] = jnp.where(lanes(rows, span) == upper_plane, ours, theirs)

        def send(k, _):
            step = k % 5
            dz = (5 - step) // 2 * (1 - 2 * (step % 2)) * sign
            other = device_at(dz, (step + k // 5 + 1) % SUBS)
            push(source.at[other], target.at[me], send_sem, recv_sem, other)
            return 0

        def send_packed(place, _):
            for kind, first in ((0, opposite), (SUBS, across)):
                push(
                    packed.at[which - 1, kind + place], packed_in.at[which - 1, kind + me % SUBS],
                    send_sem, recv_sem, first + place,
                )
            return 0

        def send_tile(other, at):
            push(source.at[other, :, at], target.at[me, :, at], send_sem, recv_sem, other)

        def send_three(k, _):
            other = (plane - 3 * sign + RINGS) % RINGS * SUBS + k // (PAIRS - 1)
            send_tile(other, columns(pair + PAIRS + 2 * upper_plane + k % (PAIRS - 1)))
            return send(k, 0)

        def send_two(k, _):
            for at in (pair + 2, next_pair + 2):
                send_tile(across + k, columns(at))
            return send(three + k, 0)

        three = SUBS * (PAIRS - 1)
        lax.fori_loop(0, SUBS, send_packed, 0)
        lax.fori_loop(0, three, send_three, 0)
        lax.fori_loop(0, SUBS, send_two, 0)
        lax.fori_loop(three + SUBS, n - three - 1, send, 0)
        target[me] = source[me]

    root_chunks = n - 3 * SUBS - 1 + 7 * SUBS // PAIRS

    ring = (3, -3, 2, -2, 1, -1)

    def wrapped(z):
        return lax.rem(z + RINGS, RINGS)

    def exchange(target, which):
        def give(k, to, owners):
            to, owners = wrapped(to), wrapped(owners)
            at = columns(lax.div(to, 2))
            held = target[pl.ds(owners * SUBS, SUBS), :, at].reshape(span, tile)
            doubled[:span], doubled[span:] = held, held
            both = doubled[...].T
            part = jnp.where(lax.rem(to, 2) == 1, both[span:], both[:span])
            part = part.reshape(SUBS, 2, rows // 2, tile)
            first = (lanes(rows // 2, span) == 0)[None]
            turned[which, k] = jnp.where(first, part[:, 0], part[:, 1])

            def send(place, _):
                push(
                    turned.at[which, k, place], crossed.at[which, k, me % SUBS],
                    cross_send.at[which], cross_recv.at[which], to * SUBS + place,
                )
                return 0

            lax.fori_loop(0, SUBS, send, 0)

        for k, dz in enumerate(ring):
            give(k, plane + dz, plane + dz + RINGS // 2)
        give(6, plane + 2 * sign, plane - sign)
        give(7, plane - sign, plane + 2 * sign)
        give(8, plane - 2 * sign, plane + sign)
        give(9, plane + sign, plane - 2 * sign)

    def place_crossed(target, which):
        arrived = crossed.at[which]
        pltpu.make_async_copy(arrived, arrived, cross_recv.at[which]).wait()
        opposite, beside = wrapped(plane + RINGS // 2), wrapped(plane - 3 * sign)
        across = wrapped(plane + 3 * sign)
        missing = columns(pair + 3 + 2 * upper_plane)
        halfway = rows // 2
        mine = lanes(rows, span) == upper_plane
        for block in range(SUBS):
            target[opposite * SUBS + block] = jnp.zeros((rows, width), jnp.float32)
            target[beside * SUBS + block, :, missing] = jnp.zeros((rows, tile), jnp.float32)
            direct = packed_in[which, block]
            for at, values in ((pair + 2, direct), (pair, pltpu.roll(direct, span, 1))):
                target[opposite * SUBS + block, :, columns(at)] = jnp.where(mine, values, 0.0)
            direct = packed_in[which, SUBS + block]
            where = across * SUBS + block
            target[where, :, columns(pair)] = jnp.where(mine, direct, 0.0)
            target[where, :, columns(pair + PAIRS + sign)] = jnp.where(mine, 0.0, direct)

        def take(k, giver, owners):
            giver = wrapped(giver)
            at, odd = columns(lax.div(giver, 2)), lax.rem(giver, 2)
            pieces = [crossed[which, k, sender] for sender in range(SUBS)]
            for block in range(SUBS):
                where = owners * SUBS + block
                top, bottom = target[where, :halfway, at], target[where, halfway:, at]
                for sender in range(SUBS):
                    shift = rows * ((sender - block) % (2 * SUBS))
                    near, far = (
                        pltpu.roll(pieces[sender], by, 1) if by else pieces[sender]
                        for by in (shift, (shift + span) % tile)
                    )
                    here = lanes(halfway, rows) == SUBS * odd + sender
                    top = jnp.where(here, jnp.where(odd == 1, far, near), top)
                    bottom = jnp.where(here, jnp.where(odd == 1, near, far), bottom)
                target[where, :halfway, at] = top
                target[where, halfway:, at] = bottom

        for k, dz in enumerate(ring):
            take(k, plane - dz, opposite)
        take(6, plane - 2 * sign, beside)
        take(7, plane - sign, beside)
        take(8, plane + 2 * sign, across)
        take(9, plane + sign, across)

    def wait_bytes(ref, sem, count=n - 1):
        some = ref.at[pl.ds(0, count)]
        pltpu.make_async_copy(some, some, sem).wait()

    def send_mixed(half, first, k, _):
        for step in range(4):
            send_grad(0, half, 4 * k + step)
        send_grad(1, 0, first + k)
        return 0

    lax.fori_loop(0, 2, functools.partial(send_mixed, 0, 0), 0)
    lax.fori_loop(0, 2, functools.partial(send_mixed, 1, 2), 0)
    for half, first in ((0, 4), (1, 0)):

        def send_rest(step, _):
            send_grad(1, half, step)
            return 0

        lax.fori_loop(first, RINGS, send_rest, 0)
    owned[n - 1] = outgoing[me]

    def invert(block, _):
        def look(slot, found):
            return jnp.where(order[0, slot] == block, slot, found)

        place[block] = lax.fori_loop(0, n, look, 0)
        return 0

    lax.fori_loop(0, blocks, invert, 0)
    grad_sum = total(jnp.sum(grad[...] * grad[...], axis=0))

    def whole(values, count=n):
        return values.reshape(count * rows, width)

    def gram_of(half):
        count = n // 2
        some_high, some_low = split(whole(owned[half * count : (half + 1) * count], count))
        turned_high, turned_low = some_high.T, some_low.T
        for part in halves(width):
            cross = dot(turned_high, some_low[:, part]) + dot(turned_low, some_high[:, part])
            yield part, dot(turned_high, some_high[:, part]) + cross

    def keep_stat(stat, parts):
        squares = jnp.zeros((1, width // 2), jnp.float32)
        for part, values in parts:
            stat[:, part] = values
            squares += jnp.sum(values * values, axis=0, keepdims=True)
        return jnp.sum(squares, axis=1, keepdims=True)

    def put_root(stat, squares, target):
        def finish(part, values):
            target[:, :, part] = values.reshape(n, rows, width // 2)

        inverse_root(stat, squares, factor, square, fourth, iterate, root, finish)

    load_right.wait()
    wait_bytes(owned, recv_grad.at[0], n // 2)
    for part, gram in gram_of(0):
        right_new[:, part] = DECAY * right_old[:, part] + (1.0 - DECAY) * gram
    wait_bytes(owned.at[pl.ds(n // 2, n // 2)], recv_grad.at[1], n // 2 - 1)
    squares = keep_stat(
        right_new,
        [
            (part, right_new[:, part] + (1.0 - DECAY) * gram)
            for part, gram in gram_of(1)
        ],
    )
    store_right_stat = pltpu.make_async_copy(right_new, right_stat_hbm, out_sems.at[1])
    store_right_stat.start()
    put_root(right_new, squares, right)
    send_root(right, right_in, 1)

    def place_rows(k, _):
        at = pl.ds(pl.multiple_of(grad_sender(k) * rows, rows), rows)
        high[at], low[at] = split(owned[k])
        return 0

    lax.fori_loop(0, n, place_rows, 0)
    load_left.wait()
    parts = []
    for part in halves(width):
        gram = dot_t(high[...], high[part]) + (
            dot_t(high[...], low[part]) + dot_t(low[...], high[part])
        )
        parts.append((part, DECAY * left_old[:, part] + (1.0 - DECAY) * gram))
    squares = keep_stat(left_new, parts)
    store_left_stat = pltpu.make_async_copy(left_new, left_stat_hbm, out_sems.at[0])
    store_left_stat.start()
    put_root(left_new, squares, left)

    def keep_split(part, values):
        right_old[:, part] = values

    other_high[...], other_low[...] = split(whole(right[...]))
    product_full(high, low, other_high, other_low, keep_split)
    high[...], low[...] = split(right_old[...])
    other_high[...], other_low[...] = split(whole(left[...]))

    def keep_precond(part, values):
        precond[:, :, part] = values.reshape(n, rows, width // 2)

    product_full(other_high, other_low, high, low, keep_precond)
    prec_sum = total(jnp.sum(precond[...] * precond[...], axis=0))
    upper = lax.broadcasted_iota(jnp.int32, norm.shape, 0) < 4
    norm[...] = jnp.where(upper, grad_sum, prec_sum)

    def share(source, target, which, device):
        pltpu.make_async_remote_copy(
            src_ref=source,
            dst_ref=target,
            send_sem=norm_send.at[which],
            recv_sem=norm_recv.at[which],
            device_id=device,
            device_id_type=MESH,
        ).start()

    def share_pre(k, _):
        share(norm_group, norm_pre.at[group], 1, {"pre": (group + k) % groups})
        return 0

    def share_train(k, _):
        share(norm_all, norm_all, 2, {"train": k})
        return 0

    @pl.when(me != 0)
    def _():
        share(norm, norm_train.at[me], 0, {"train": 0})

    send_root(left, left_in, 2)

    @pl.when(me == 0)
    def _():
        norm_train[0] = norm[...]
        wait_bytes(norm_train, norm_recv.at[0])
        norm_group[...] = jnp.sum(norm_train[...], axis=0)
        lax.fori_loop(1, groups, share_pre, 0)
        norm_pre[group] = norm_group[...]

    wait_bytes(right_in, recv_sems.at[1], root_chunks)
    exchange(right_in, 0)
    send_part(precond, precond_in, 3, 0, n * 7 // 16)

    @pl.when(me == 0)
    def _():
        wait_bytes(norm_pre, norm_recv.at[1], groups - 1)
        wait_bytes(norm_pre, norm_send.at[1], groups - 1)
        norm_all[...] = jnp.sum(norm_pre[...], axis=0)
        lax.fori_loop(1, n, share_train, 0)

    wait_bytes(left_in, recv_sems.at[2], root_chunks)
    exchange(left_in, 1)
    send_part(precond, precond_in, 3, n * 7 // 16, n - 1)
    keep_own = pltpu.make_async_copy(precond.at[me], precond_in.at[me], out_sems.at[4])
    keep_own.start()

    def to_blocks(source, target, which):
        def move(block, _):
            ready[which, block] = source[place[block]]
            return 0

        lax.fori_loop(0, blocks, move, 0)
        store = pltpu.make_async_copy(ready.at[which], target, out_sems.at[2 + which])
        store.start()
        return store

    place_crossed(right_in, 0)
    store_right = to_blocks(right_in, right_root_hbm, 1)
    place_crossed(left_in, 1)
    store_left = to_blocks(left_in, left_root_hbm, 0)

    @pl.when(me != 0)
    def _():
        pltpu.make_async_copy(norm, norm, norm_send.at[0]).wait()
        pltpu.make_async_copy(norm_all, norm_all, norm_recv.at[2]).wait()

    @pl.when(me == 0)
    def _():
        wait_bytes(norm_train, norm_send.at[2])

    store_norm = pltpu.make_async_copy(norm_all, norm_hbm, out_sems.at[5])
    store_norm.start()
    wait_bytes(owned, send_sems.at[0])
    wait_bytes(right, send_sems.at[1], root_chunks)
    wait_bytes(left, send_sems.at[2], root_chunks)
    for which in range(2):
        pltpu.make_async_copy(turned.at[which], turned.at[which], cross_send.at[which]).wait()
    wait_bytes(precond, send_sems.at[3])
    store_left_stat.wait()
    store_right_stat.wait()
    store_left.wait()
    store_right.wait()
    store_norm.wait()
    keep_own.wait()
    wait_bytes(precond_in, recv_sems.at[3])


def in_hbm(value):
    return pltpu.with_memory_space_constraint(value, pltpu.HBM)


def copy_in_parts(source, target, sems):
    count = source.shape[0] // 4
    parts = [pl.ds(part * count, count) for part in range(4)]
    copies = [
        pltpu.make_async_copy(source.at[at], target.at[at], sems.at[part])
        for part, at in enumerate(parts)
    ]
    for copy in copies:
        copy.start()
    return copies


def deliver(
    order_hbm, precond_hbm, left, right, left_stat, right_stat, norm_hbm,
    update, left_out, right_out, left_stat_out, right_stat_out,
    precond, norm, order, in_sems, out_sems,
):
    blocks = precond.shape[0]
    load_order = pltpu.make_async_copy(order_hbm, order, in_sems.at[4])
    load_norm = pltpu.make_async_copy(norm_hbm, norm, in_sems.at[5])
    load_order.start()
    load_norm.start()
    loads = copy_in_parts(precond_hbm, precond, in_sems)
    pairs = ((left, left_out), (right, right_out), (left_stat, left_stat_out), (right_stat, right_stat_out))
    stores = []
    for i, (source, target) in enumerate(pairs):
        stores += copy_in_parts(source, target, out_sems.at[pl.ds(4 * i, 4)])
    load_order.wait()
    load_norm.wait()
    graft = jnp.sqrt(norm[0:1, 0:1] / (norm[4:5, 0:1] + 1e-6))

    def scale(slot, _):
        precond[slot] = precond[slot] * graft
        pltpu.make_async_copy(
            precond.at[slot], update.at[order[0, slot]], out_sems.at[16]
        ).start()
        return 0

    for part, load in enumerate(loads):
        load.wait()
        lax.fori_loop(part * (blocks // 4), (part + 1) * (blocks // 4), scale, 0)
    for store in stores:
        store.wait()
    pltpu.make_async_copy(precond, update, out_sems.at[16]).wait()


def shards(gradient, assignment, left_prev, right_prev):
    n, groups = lax.axis_size("train"), lax.axis_size("pre")
    blocks, rows, width = gradient.shape
    pieces = jax.ShapeDtypeStruct((blocks, rows, width), jnp.float32)
    square = jax.ShapeDtypeStruct((width, width), jnp.float32)
    any_space = pl.BlockSpec(memory_space=pl.ANY)
    pieces_vmem = pltpu.VMEM(pieces.shape, jnp.float32)
    square_vmem = pltpu.VMEM(square.shape, jnp.float32)
    square_half = pltpu.VMEM(square.shape, jnp.bfloat16)
    results = (pieces, pieces, pieces, square, square)
    made = pl.pallas_call(
        body,
        out_shape=results + (jax.ShapeDtypeStruct((8, 128), jnp.float32),),
        in_specs=[pl.BlockSpec(memory_space=pltpu.HBM)] * 4,
        out_specs=(any_space,) * 6,
        scratch_shapes=[pieces_vmem] * 3
        + [square_vmem] * 4
        + [pieces_vmem] * 5
        + [
            pltpu.VMEM((2,) + pieces.shape, jnp.float32),
            pltpu.VMEM((2, 2 * SUBS, rows, width // PAIRS), jnp.float32),
            pltpu.VMEM((2, 2 * SUBS, rows, width // PAIRS), jnp.float32),
            pltpu.VMEM((2, 10, SUBS, rows // 2, width // PAIRS), jnp.float32),
            pltpu.VMEM((2, 10, SUBS, rows // 2, width // PAIRS), jnp.float32),
            pltpu.VMEM((width // PAIRS, width // PAIRS), jnp.float32),
        ]
        + [square_half] * 4
        + [
            pltpu.VMEM((ITERS,) + square.shape, jnp.bfloat16),
            square_half,
            square_half,
            pltpu.VMEM((ITERS - 1,) + square.shape, jnp.bfloat16),
            pltpu.VMEM((ITERS - 1,) + square.shape, jnp.bfloat16),
            pltpu.VMEM((8, 128), jnp.float32),
            pltpu.VMEM((8, 128), jnp.float32),
            pltpu.VMEM((8, 128), jnp.float32),
            pltpu.VMEM((groups, 8, 128), jnp.float32),
            pltpu.VMEM((n, 8, 128), jnp.float32),
            pltpu.SMEM((1, blocks), jnp.int32),
            pltpu.SMEM((blocks,), jnp.int32),
            pltpu.SemaphoreType.DMA((8,)),
            pltpu.SemaphoreType.DMA((6,)),
            pltpu.SemaphoreType.DMA((4,)),
            pltpu.SemaphoreType.DMA((2,)),
            pltpu.SemaphoreType.DMA((4,)),
            pltpu.SemaphoreType.DMA((2,)),
            pltpu.SemaphoreType.DMA((2,)),
            pltpu.SemaphoreType.DMA((3,)),
            pltpu.SemaphoreType.DMA((3,)),
        ],
        compiler_params=pltpu.CompilerParams(
            collective_id=0, has_side_effects=True, vmem_limit_bytes=48 * 2**20
        ),
        cost_estimate=pl.CostEstimate(
            flops=2 * 28 * width**3, bytes_accessed=32 * width**2, transcendentals=0
        ),
        name="shampoo",
    )(*(in_hbm(value) for value in (assignment, gradient, left_prev[0, 0], right_prev[0, 0])))
    update, left_root, right_root, left_stat, right_stat = pl.pallas_call(
        deliver,
        out_shape=results,
        in_specs=[any_space] * 7,
        out_specs=(pl.BlockSpec(memory_space=pltpu.HBM),) * 5,
        scratch_shapes=[
            pieces_vmem,
            pltpu.VMEM((8, 128), jnp.float32),
            pltpu.SMEM((1, blocks), jnp.int32),
            pltpu.SemaphoreType.DMA((6,)),
            pltpu.SemaphoreType.DMA((17,)),
        ],
        compiler_params=pltpu.CompilerParams(vmem_limit_bytes=4 * 2**20),
        name="deliver",
    )(in_hbm(assignment), *made)
    return update, left_root, right_root, left_stat[None, None], right_stat[None, None]


def solution(mesh):
    by_rows = P("pre", "train", None)
    by_owner = P("pre", "train", None, None)
    return jax.shard_map(
        shards,
        mesh=mesh,
        in_specs=(by_rows, P("pre", None), by_owner, by_owner),
        out_specs=(by_rows, by_rows, by_rows, by_owner, by_owner),
        check_vma=False,
    )
```

```python
import functools

import jax
import jax.numpy as jnp
from jax import lax
from jax.experimental import pallas as pl
from jax.experimental.pallas import tpu as pltpu
from jax.sharding import PartitionSpec as P

MESH = pl.DeviceIdType.MESH
DECAY = 0.95
ITERS = 3
RINGS = 8
SUBS = 4
PAIRS = 4


def split(values):
    high = values.astype(jnp.bfloat16)
    low = (values - high.astype(jnp.float32)).astype(jnp.bfloat16)
    return high, low


def dot(left, right):
    return jnp.dot(left, right, preferred_element_type=jnp.float32)


def dot_t(left, right):
    return lax.dot_general(
        left, right, (((1,), (1,)), ((), ())), preferred_element_type=jnp.float32
    )


def total(values):
    return jnp.sum(jnp.sum(values, axis=0, keepdims=True), axis=1, keepdims=True)


def halves(width):
    return [slice(start, start + width // 2) for start in (0, width // 2)]


def product(left, right, finish):
    for part in halves(right.shape[1]):
        finish(part, dot(left[...], right[:, part]))


def product_full(left_high, left_low, right_high, right_low, finish):
    for part in halves(right_high.shape[1]):
        cross = dot(left_high[...], right_low[:, part]) + dot(left_low[...], right_high[:, part])
        finish(part, dot(left_high[...], right_high[:, part]) + cross)


def keep(target):
    def finish(part, values):
        target[:, part] = values.astype(target.dtype)

    return finish


def put_factor(factor, part, iterate):
    for rows in halves(factor.shape[0]):
        values = -0.25 * iterate[rows]
        if rows == part:
            shape = values.shape
            diagonal = lax.broadcasted_iota(jnp.int32, shape, 0) == lax.broadcasted_iota(
                jnp.int32, shape, 1
            )
            values = jnp.where(diagonal, 1.25 + values, values)
        factor[rows, part] = values.astype(jnp.bfloat16)


def inverse_root(stat, squares, factor, square, fourth, iterate, root, finish):
    scale = 2.5 / jnp.sqrt(squares)
    start = jnp.sqrt(jnp.sqrt(scale)).astype(jnp.bfloat16).astype(jnp.float32)
    for part in halves(stat.shape[1]):
        values = scale * stat[:, part]
        iterate[0, :, part] = values.astype(jnp.bfloat16)
        put_factor(factor.at[0], part, values)
        root[0, :, part] = (start * factor[0, :, part].astype(jnp.float32)).astype(jnp.bfloat16)

    def advance(now, last):
        def finish_iterate(part, values):
            if not last:
                iterate[now + 1, :, part] = values.astype(jnp.bfloat16)
            put_factor(factor.at[now + 1], part, values)

        product(factor.at[now], factor.at[now], keep(square))
        product(square, square, keep(fourth))
        product(fourth, iterate.at[now], finish_iterate)

    advance(0, False)
    product(root.at[0], factor.at[1], keep(root.at[1]))
    advance(1, True)
    product(root.at[1], factor.at[2], finish)


def body(
    order_hbm, grad_hbm, left_prev, right_prev,
    precond_in, left_root_hbm, right_root_hbm, left_stat_hbm, right_stat_hbm, norm_hbm,
    grad, outgoing, owned, left_old, right_old, left_new, right_new,
    left, right, precond, left_in, right_in, ready, packed, packed_in, turned, crossed, doubled,
    high, low, other_high, other_low, factor, square, fourth, iterate, root,
    norm, norm_group, norm_all, norm_pre, norm_train, order, place,
    in_sems, out_sems, send_sems, recv_grad, recv_sems,
    cross_send, cross_recv, norm_send, norm_recv,
):
    me, group = lax.axis_index("train"), lax.axis_index("pre")
    n, groups = lax.axis_size("train"), lax.axis_size("pre")
    blocks, rows, width = grad.shape
    plane, y_at, core_at = me // SUBS, (me // 2) % 2, me % 2
    pair, upper_plane, peers = plane // 2, plane % 2, n // PAIRS
    tile = width // PAIRS

    barrier = pltpu.get_barrier_semaphore()

    load_left = pltpu.make_async_copy(left_prev, left_old, in_sems.at[1])
    load_right = pltpu.make_async_copy(right_prev, right_old, in_sems.at[2])
    load_order = pltpu.make_async_copy(order_hbm, order, in_sems.at[3])
    load_order.start()
    load_grad = copy_in_parts(grad_hbm, grad, in_sems.at[pl.ds(4, 4)])
    load_left.start()
    load_right.start()
    def greet_train(k, _):
        pl.semaphore_signal(
            barrier, inc=1, device_id={"train": (me + k) % n}, device_id_type=MESH
        )
        return 0

    def greet_pre(k, _):
        pl.semaphore_signal(
            barrier, inc=1, device_id={"pre": (group + k) % groups}, device_id_type=MESH
        )
        return 0

    lax.fori_loop(1, n, greet_train, 0)

    @pl.when(me == 0)
    def _():
        lax.fori_loop(1, groups, greet_pre, 0)

    load_order.wait()
    for load in load_grad:
        load.wait()

    def pick(slot, _):
        outgoing[slot] = grad[order[0, slot]]
        return 0

    lax.fori_loop(0, n, pick, 0)
    pl.semaphore_wait(barrier, n - 1 + jnp.where(me == 0, groups - 1, 0))

    def away(step, core):
        return (RINGS - step) // 2 * (2 * (step % 2) - 1) * (1 - 2 * core)

    def device_at(dz, sub):
        z = (plane + dz + RINGS) % RINGS
        return (z * 2 + (y_at + sub // 2) % 2) * 2 + (core_at + sub) % 2

    def push(source, target, send_sem, recv_sem, other):
        pltpu.make_async_remote_copy(
            src_ref=source,
            dst_ref=target,
            send_sem=send_sem,
            recv_sem=recv_sem,
            device_id={"train": other},
            device_id_type=MESH,
        ).start()

    def send_grad(core, half, step):
        across = (half + step) % 2
        other_core = (core_at + core) % 2
        other = device_at(away(step, core_at), 2 * across + other_core)
        at = half * (n // 2) + 2 * step + 1 - other_core

        @pl.when(other != me)
        def _():
            push(outgoing.at[other], owned.at[at], send_sems.at[0], recv_grad.at[half], other)

    def grad_sender(slot):
        half, step, other_core = slot // (n // 2), slot % (n // 2) // 2, 1 - slot % 2
        dz = away(step, (core_at + other_core) % 2)
        return device_at(-dz, 2 * ((half + step) % 2) + other_core)

    def send_part(source, target, which, first, last):
        def send(k, _):
            step = k % RINGS
            other = device_at(away(step, core_at), (step + k // RINGS + 2) % SUBS)
            push(source.at[other], target.at[me], send_sems.at[which], recv_sems.at[which], other)
            return 0

        lax.fori_loop(first, last, send, 0)

    def columns(which_pair):
        return pl.ds(pl.multiple_of(lax.rem(which_pair, PAIRS) * tile, tile), tile)

    sign = 1 - 2 * upper_plane
    span = SUBS * rows

    def lanes(count, size):
        return lax.broadcasted_iota(jnp.int32, (count, tile), 1) // size

    def send_root(source, target, which):
        send_sem, recv_sem = send_sems.at[which], recv_sems.at[which]
        opposite = (plane + RINGS // 2) % RINGS * SUBS
        across = (plane + 3 * sign + RINGS) % RINGS * SUBS
        next_pair = pair + PAIRS + sign
        for place in range(SUBS):
            ours = source[across + place, :, columns(pair)]
            theirs = source[across + place, :, columns(next_pair)]
            packed[which - 1, SUBS + place] = jnp.where(
                lanes(rows, span) == upper_plane, ours, theirs
            )
            ours = source[opposite + place, :, columns(pair)]
            theirs = pltpu.roll(source[opposite + place, :, columns(pair + 2)], span, 1)
            packed[which - 1, place] = jnp.where(lanes(rows, span) == upper_plane, ours, theirs)

        def send(k, _):
            step = k % 5
            dz = (5 - step) // 2 * (1 - 2 * (step % 2)) * sign
            other = device_at(dz, (step + k // 5 + 1) % SUBS)
            push(source.at[other], target.at[me], send_sem, recv_sem, other)
            return 0

        def send_packed(place, _):
            for kind, first in ((0, opposite), (SUBS, across)):
                push(
                    packed.at[which - 1, kind + place], packed_in.at[which - 1, kind + me % SUBS],
                    send_sem, recv_sem, first + place,
                )
            return 0

        def send_tile(other, at):
            push(source.at[other, :, at], target.at[me, :, at], send_sem, recv_sem, other)

        def send_three(k, _):
            other = (plane - 3 * sign + RINGS) % RINGS * SUBS + k // (PAIRS - 1)
            send_tile(other, columns(pair + PAIRS + 2 * upper_plane + k % (PAIRS - 1)))
            return send(k, 0)

        def send_two(k, _):
            for at in (pair + 2, next_pair + 2):
                send_tile(across + k, columns(at))
            return send(three + k, 0)

        three = SUBS * (PAIRS - 1)
        lax.fori_loop(0, SUBS, send_packed, 0)
        lax.fori_loop(0, three, send_three, 0)
        lax.fori_loop(0, SUBS, send_two, 0)
        lax.fori_loop(three + SUBS, n - three - 1, send, 0)
        target[me] = source[me]

    root_chunks = n - 3 * SUBS - 1 + 7 * SUBS // PAIRS

    ring = (3, -3, 2, -2, 1, -1)

    def wrapped(z):
        return lax.rem(z + RINGS, RINGS)

    def exchange(target, which):
        def give(k, to, owners):
            to, owners = wrapped(to), wrapped(owners)
            at = columns(lax.div(to, 2))
            held = target[pl.ds(owners * SUBS, SUBS), :, at].reshape(span, tile)
            doubled[:span], doubled[span:] = held, held
            both = doubled[...].T
            part = jnp.where(lax.rem(to, 2) == 1, both[span:], both[:span])
            part = part.reshape(SUBS, 2, rows // 2, tile)
            first = (lanes(rows // 2, span) == 0)[None]
            turned[which, k] = jnp.where(first, part[:, 0], part[:, 1])

            def send(place, _):
                push(
                    turned.at[which, k, place], crossed.at[which, k, me % SUBS],
                    cross_send.at[which], cross_recv.at[which], to * SUBS + place,
                )
                return 0

            lax.fori_loop(0, SUBS, send, 0)

        for k, dz in enumerate(ring):
            give(k, plane + dz, plane + dz + RINGS // 2)
        give(6, plane + 2 * sign, plane - sign)
        give(7, plane - sign, plane + 2 * sign)
        give(8, plane - 2 * sign, plane + sign)
        give(9, plane + sign, plane - 2 * sign)

    def place_crossed(target, which):
        arrived = crossed.at[which]
        pltpu.make_async_copy(arrived, arrived, cross_recv.at[which]).wait()
        opposite, beside = wrapped(plane + RINGS // 2), wrapped(plane - 3 * sign)
        across = wrapped(plane + 3 * sign)
        missing = columns(pair + 3 + 2 * upper_plane)
        halfway = rows // 2
        mine = lanes(rows, span) == upper_plane
        for block in range(SUBS):
            target[opposite * SUBS + block] = jnp.zeros((rows, width), jnp.float32)
            target[beside * SUBS + block, :, missing] = jnp.zeros((rows, tile), jnp.float32)
            direct = packed_in[which, block]
            for at, values in ((pair + 2, direct), (pair, pltpu.roll(direct, span, 1))):
                target[opposite * SUBS + block, :, columns(at)] = jnp.where(mine, values, 0.0)
            direct = packed_in[which, SUBS + block]
            where = across * SUBS + block
            target[where, :, columns(pair)] = jnp.where(mine, direct, 0.0)
            target[where, :, columns(pair + PAIRS + sign)] = jnp.where(mine, 0.0, direct)

        def take(k, giver, owners):
            giver = wrapped(giver)
            at, odd = columns(lax.div(giver, 2)), lax.rem(giver, 2)
            pieces = [crossed[which, k, sender] for sender in range(SUBS)]
            for block in range(SUBS):
                where = owners * SUBS + block
                top, bottom = target[where, :halfway, at], target[where, halfway:, at]
                for sender in range(SUBS):
                    shift = rows * ((sender - block) % (2 * SUBS))
                    near, far = (
                        pltpu.roll(pieces[sender], by, 1) if by else pieces[sender]
                        for by in (shift, (shift + span) % tile)
                    )
                    here = lanes(halfway, rows) == SUBS * odd + sender
                    top = jnp.where(here, jnp.where(odd == 1, far, near), top)
                    bottom = jnp.where(here, jnp.where(odd == 1, near, far), bottom)
                target[where, :halfway, at] = top
                target[where, halfway:, at] = bottom

        for k, dz in enumerate(ring):
            take(k, plane - dz, opposite)
        take(6, plane - 2 * sign, beside)
        take(7, plane - sign, beside)
        take(8, plane + 2 * sign, across)
        take(9, plane + sign, across)

    def wait_bytes(ref, sem, count=n - 1):
        some = ref.at[pl.ds(0, count)]
        pltpu.make_async_copy(some, some, sem).wait()

    def send_mixed(half, first, k, _):
        for step in range(4):
            send_grad(0, half, 4 * k + step)
        send_grad(1, 0, first + k)
        return 0

    lax.fori_loop(0, 2, functools.partial(send_mixed, 0, 0), 0)
    lax.fori_loop(0, 2, functools.partial(send_mixed, 1, 2), 0)
    for half, first in ((0, 4), (1, 0)):

        def send_rest(step, _):
            send_grad(1, half, step)
            return 0

        lax.fori_loop(first, RINGS, send_rest, 0)
    owned[n - 1] = outgoing[me]

    def invert(block, _):
        def look(slot, found):
            return jnp.where(order[0, slot] == block, slot, found)

        place[block] = lax.fori_loop(0, n, look, 0)
        return 0

    lax.fori_loop(0, blocks, invert, 0)
    grad_sum = total(jnp.sum(grad[...] * grad[...], axis=0))

    def whole(values, count=n):
        return values.reshape(count * rows, width)

    def gram_of(half):
        count = n // 2
        some_high, some_low = split(whole(owned[half * count : (half + 1) * count], count))
        turned_high, turned_low = some_high.T, some_low.T
        for part in halves(width):
            cross = dot(turned_high, some_low[:, part]) + dot(turned_low, some_high[:, part])
            yield part, dot(turned_high, some_high[:, part]) + cross

    def keep_stat(stat, parts):
        squares = jnp.zeros((1, width // 2), jnp.float32)
        for part, values in parts:
            stat[:, part] = values
            squares += jnp.sum(values * values, axis=0, keepdims=True)
        return jnp.sum(squares, axis=1, keepdims=True)

    def put_root(stat, squares, target):
        def finish(part, values):
            target[:, :, part] = values.reshape(n, rows, width // 2)

        inverse_root(stat, squares, factor, square, fourth, iterate, root, finish)

    load_right.wait()
    wait_bytes(owned, recv_grad.at[0], n // 2)
    for part, gram in gram_of(0):
        right_new[:, part] = DECAY * right_old[:, part] + (1.0 - DECAY) * gram
    wait_bytes(owned.at[pl.ds(n // 2, n // 2)], recv_grad.at[1], n // 2 - 1)
    squares = keep_stat(
        right_new,
        [
            (part, right_new[:, part] + (1.0 - DECAY) * gram)
            for part, gram in gram_of(1)
        ],
    )
    store_right_stat = pltpu.make_async_copy(right_new, right_stat_hbm, out_sems.at[1])
    store_right_stat.start()
    put_root(right_new, squares, right)
    send_root(right, right_in, 1)

    def place_rows(k, _):
        at = pl.ds(pl.multiple_of(grad_sender(k) * rows, rows), rows)
        high[at], low[at] = split(owned[k])
        return 0

    lax.fori_loop(0, n, place_rows, 0)
    load_left.wait()
    parts = []
    for part in halves(width):
        gram = dot_t(high[...], high[part]) + (
            dot_t(high[...], low[part]) + dot_t(low[...], high[part])
        )
        parts.append((part, DECAY * left_old[:, part] + (1.0 - DECAY) * gram))
    squares = keep_stat(left_new, parts)
    store_left_stat = pltpu.make_async_copy(left_new, left_stat_hbm, out_sems.at[0])
    store_left_stat.start()
    put_root(left_new, squares, left)

    def keep_split(part, values):
        right_old[:, part] = values

    other_high[...], other_low[...] = split(whole(right[...]))
    product_full(high, low, other_high, other_low, keep_split)
    high[...], low[...] = split(right_old[...])
    other_high[...], other_low[...] = split(whole(left[...]))

    def keep_precond(part, values):
        precond[:, :, part] = values.reshape(n, rows, width // 2)

    product_full(other_high, other_low, high, low, keep_precond)
    prec_sum = total(jnp.sum(precond[...] * precond[...], axis=0))
    upper = lax.broadcasted_iota(jnp.int32, norm.shape, 0) < 4
    norm[...] = jnp.where(upper, grad_sum, prec_sum)

    def share(source, target, which, device):
        pltpu.make_async_remote_copy(
            src_ref=source,
            dst_ref=target,
            send_sem=norm_send.at[which],
            recv_sem=norm_recv.at[which],
            device_id=device,
            device_id_type=MESH,
        ).start()

    def share_pre(k, _):
        share(norm_group, norm_pre.at[group], 1, {"pre": (group + k) % groups})
        return 0

    def share_train(k, _):
        share(norm_all, norm_all, 2, {"train": k})
        return 0

    @pl.when(me != 0)
    def _():
        share(norm, norm_train.at[me], 0, {"train": 0})

    send_root(left, left_in, 2)

    @pl.when(me == 0)
    def _():
        norm_train[0] = norm[...]
        wait_bytes(norm_train, norm_recv.at[0])
        norm_group[...] = jnp.sum(norm_train[...], axis=0)
        lax.fori_loop(1, groups, share_pre, 0)
        norm_pre[group] = norm_group[...]

    wait_bytes(right_in, recv_sems.at[1], root_chunks)
    exchange(right_in, 0)
    send_part(precond, precond_in, 3, 0, n * 11 // 16)

    @pl.when(me == 0)
    def _():
        wait_bytes(norm_pre, norm_recv.at[1], groups - 1)
        wait_bytes(norm_pre, norm_send.at[1], groups - 1)
        norm_all[...] = jnp.sum(norm_pre[...], axis=0)
        lax.fori_loop(1, n, share_train, 0)

    wait_bytes(left_in, recv_sems.at[2], root_chunks)
    exchange(left_in, 1)
    send_part(precond, precond_in, 3, n * 11 // 16, n - 1)
    keep_own = pltpu.make_async_copy(precond.at[me], precond_in.at[me], out_sems.at[4])
    keep_own.start()

    def to_blocks(source, target, which):
        def move(block, _):
            ready[which, block] = source[place[block]]
            return 0

        lax.fori_loop(0, blocks, move, 0)
        store = pltpu.make_async_copy(ready.at[which], target, out_sems.at[2 + which])
        store.start()
        return store

    place_crossed(right_in, 0)
    store_right = to_blocks(right_in, right_root_hbm, 1)
    place_crossed(left_in, 1)
    store_left = to_blocks(left_in, left_root_hbm, 0)

    @pl.when(me != 0)
    def _():
        pltpu.make_async_copy(norm, norm, norm_send.at[0]).wait()
        pltpu.make_async_copy(norm_all, norm_all, norm_recv.at[2]).wait()

    @pl.when(me == 0)
    def _():
        wait_bytes(norm_train, norm_send.at[2])

    store_norm = pltpu.make_async_copy(norm_all, norm_hbm, out_sems.at[5])
    store_norm.start()
    wait_bytes(owned, send_sems.at[0])
    wait_bytes(right, send_sems.at[1], root_chunks)
    wait_bytes(left, send_sems.at[2], root_chunks)
    for which in range(2):
        pltpu.make_async_copy(turned.at[which], turned.at[which], cross_send.at[which]).wait()
    wait_bytes(precond, send_sems.at[3])
    store_left_stat.wait()
    store_right_stat.wait()
    store_left.wait()
    store_right.wait()
    store_norm.wait()
    keep_own.wait()
    wait_bytes(precond_in, recv_sems.at[3])


def in_hbm(value):
    return pltpu.with_memory_space_constraint(value, pltpu.HBM)


def copy_in_parts(source, target, sems):
    count = source.shape[0] // 4
    parts = [pl.ds(part * count, count) for part in range(4)]
    copies = [
        pltpu.make_async_copy(source.at[at], target.at[at], sems.at[part])
        for part, at in enumerate(parts)
    ]
    for copy in copies:
        copy.start()
    return copies


def deliver(
    order_hbm, precond_hbm, left, right, left_stat, right_stat, norm_hbm,
    update, left_out, right_out, left_stat_out, right_stat_out,
    precond, norm, order, in_sems, out_sems,
):
    blocks = precond.shape[0]
    load_order = pltpu.make_async_copy(order_hbm, order, in_sems.at[4])
    load_norm = pltpu.make_async_copy(norm_hbm, norm, in_sems.at[5])
    load_order.start()
    load_norm.start()
    loads = copy_in_parts(precond_hbm, precond, in_sems)
    pairs = ((left, left_out), (right, right_out), (left_stat, left_stat_out), (right_stat, right_stat_out))
    stores = []
    for i, (source, target) in enumerate(pairs):
        stores += copy_in_parts(source, target, out_sems.at[pl.ds(4 * i, 4)])
    load_order.wait()
    load_norm.wait()
    graft = jnp.sqrt(norm[0:1, 0:1] / (norm[4:5, 0:1] + 1e-6))

    def scale(slot, _):
        precond[slot] = precond[slot] * graft
        pltpu.make_async_copy(
            precond.at[slot], update.at[order[0, slot]], out_sems.at[16]
        ).start()
        return 0

    for part, load in enumerate(loads):
        load.wait()
        lax.fori_loop(part * (blocks // 4), (part + 1) * (blocks // 4), scale, 0)
    for store in stores:
        store.wait()
    pltpu.make_async_copy(precond, update, out_sems.at[16]).wait()


def shards(gradient, assignment, left_prev, right_prev):
    n, groups = lax.axis_size("train"), lax.axis_size("pre")
    blocks, rows, width = gradient.shape
    pieces = jax.ShapeDtypeStruct((blocks, rows, width), jnp.float32)
    square = jax.ShapeDtypeStruct((width, width), jnp.float32)
    any_space = pl.BlockSpec(memory_space=pl.ANY)
    pieces_vmem = pltpu.VMEM(pieces.shape, jnp.float32)
    square_vmem = pltpu.VMEM(square.shape, jnp.float32)
    square_half = pltpu.VMEM(square.shape, jnp.bfloat16)
    results = (pieces, pieces, pieces, square, square)
    made = pl.pallas_call(
        body,
        out_shape=results + (jax.ShapeDtypeStruct((8, 128), jnp.float32),),
        in_specs=[pl.BlockSpec(memory_space=pltpu.HBM)] * 4,
        out_specs=(any_space,) * 6,
        scratch_shapes=[pieces_vmem] * 3
        + [square_vmem] * 4
        + [pieces_vmem] * 5
        + [
            pltpu.VMEM((2,) + pieces.shape, jnp.float32),
            pltpu.VMEM((2, 2 * SUBS, rows, width // PAIRS), jnp.float32),
            pltpu.VMEM((2, 2 * SUBS, rows, width // PAIRS), jnp.float32),
            pltpu.VMEM((2, 10, SUBS, rows // 2, width // PAIRS), jnp.float32),
            pltpu.VMEM((2, 10, SUBS, rows // 2, width // PAIRS), jnp.float32),
            pltpu.VMEM((width // PAIRS, width // PAIRS), jnp.float32),
        ]
        + [square_half] * 4
        + [
            pltpu.VMEM((ITERS,) + square.shape, jnp.bfloat16),
            square_half,
            square_half,
            pltpu.VMEM((ITERS - 1,) + square.shape, jnp.bfloat16),
            pltpu.VMEM((ITERS - 1,) + square.shape, jnp.bfloat16),
            pltpu.VMEM((8, 128), jnp.float32),
            pltpu.VMEM((8, 128), jnp.float32),
            pltpu.VMEM((8, 128), jnp.float32),
            pltpu.VMEM((groups, 8, 128), jnp.float32),
            pltpu.VMEM((n, 8, 128), jnp.float32),
            pltpu.SMEM((1, blocks), jnp.int32),
            pltpu.SMEM((blocks,), jnp.int32),
            pltpu.SemaphoreType.DMA((8,)),
            pltpu.SemaphoreType.DMA((6,)),
            pltpu.SemaphoreType.DMA((4,)),
            pltpu.SemaphoreType.DMA((2,)),
            pltpu.SemaphoreType.DMA((4,)),
            pltpu.SemaphoreType.DMA((2,)),
            pltpu.SemaphoreType.DMA((2,)),
            pltpu.SemaphoreType.DMA((3,)),
            pltpu.SemaphoreType.DMA((3,)),
        ],
        compiler_params=pltpu.CompilerParams(
            collective_id=0, has_side_effects=True, vmem_limit_bytes=48 * 2**20
        ),
        cost_estimate=pl.CostEstimate(
            flops=2 * 28 * width**3, bytes_accessed=32 * width**2, transcendentals=0
        ),
        name="shampoo",
    )(*(in_hbm(value) for value in (assignment, gradient, left_prev[0, 0], right_prev[0, 0])))
    update, left_root, right_root, left_stat, right_stat = pl.pallas_call(
        deliver,
        out_shape=results,
        in_specs=[any_space] * 7,
        out_specs=(pl.BlockSpec(memory_space=pltpu.HBM),) * 5,
        scratch_shapes=[
            pieces_vmem,
            pltpu.VMEM((8, 128), jnp.float32),
            pltpu.SMEM((1, blocks), jnp.int32),
            pltpu.SemaphoreType.DMA((6,)),
            pltpu.SemaphoreType.DMA((17,)),
        ],
        compiler_params=pltpu.CompilerParams(vmem_limit_bytes=4 * 2**20),
        name="deliver",
    )(in_hbm(assignment), *made)
    return update, left_root, right_root, left_stat[None, None], right_stat[None, None]


def solution(mesh):
    by_rows = P("pre", "train", None)
    by_owner = P("pre", "train", None, None)
    return jax.shard_map(
        shards,
        mesh=mesh,
        in_specs=(by_rows, P("pre", None), by_owner, by_owner),
        out_specs=(by_rows, by_rows, by_rows, by_owner, by_owner),
        check_vma=False,
    )
```

```python
import functools

import jax
import jax.numpy as jnp
from jax import lax
from jax.experimental import pallas as pl
from jax.experimental.pallas import tpu as pltpu
from jax.sharding import PartitionSpec as P

MESH = pl.DeviceIdType.MESH
DECAY = 0.95
ITERS = 3
RINGS = 8
SUBS = 4
PAIRS = 4


def split(values):
    high = values.astype(jnp.bfloat16)
    low = (values - high.astype(jnp.float32)).astype(jnp.bfloat16)
    return high, low


def dot(left, right):
    return jnp.dot(left, right, preferred_element_type=jnp.float32)


def dot_t(left, right):
    return lax.dot_general(
        left, right, (((1,), (1,)), ((), ())), preferred_element_type=jnp.float32
    )


def total(values):
    return jnp.sum(jnp.sum(values, axis=0, keepdims=True), axis=1, keepdims=True)


def halves(width):
    return [slice(start, start + width // 2) for start in (0, width // 2)]


def product(left, right, finish):
    for part in halves(right.shape[1]):
        finish(part, dot(left[...], right[:, part]))


def product_full(left_high, left_low, right_high, right_low, finish):
    for part in halves(right_high.shape[1]):
        cross = dot(left_high[...], right_low[:, part]) + dot(left_low[...], right_high[:, part])
        finish(part, dot(left_high[...], right_high[:, part]) + cross)


def keep(target):
    def finish(part, values):
        target[:, part] = values.astype(target.dtype)

    return finish


def put_factor(factor, part, iterate):
    for rows in halves(factor.shape[0]):
        values = -0.25 * iterate[rows]
        if rows == part:
            shape = values.shape
            diagonal = lax.broadcasted_iota(jnp.int32, shape, 0) == lax.broadcasted_iota(
                jnp.int32, shape, 1
            )
            values = jnp.where(diagonal, 1.25 + values, values)
        factor[rows, part] = values.astype(jnp.bfloat16)


def inverse_root(stat, squares, factor, square, fourth, iterate, root, finish):
    scale = 2.5 / jnp.sqrt(squares)
    start = jnp.sqrt(jnp.sqrt(scale)).astype(jnp.bfloat16).astype(jnp.float32)
    for part in halves(stat.shape[1]):
        values = scale * stat[:, part]
        iterate[0, :, part] = values.astype(jnp.bfloat16)
        put_factor(factor.at[0], part, values)
        root[0, :, part] = (start * factor[0, :, part].astype(jnp.float32)).astype(jnp.bfloat16)

    def advance(now, last):
        def finish_iterate(part, values):
            if not last:
                iterate[now + 1, :, part] = values.astype(jnp.bfloat16)
            put_factor(factor.at[now + 1], part, values)

        product(factor.at[now], factor.at[now], keep(square))
        product(square, square, keep(fourth))
        product(fourth, iterate.at[now], finish_iterate)

    advance(0, False)
    product(root.at[0], factor.at[1], keep(root.at[1]))
    advance(1, True)
    product(root.at[1], factor.at[2], finish)


def body(
    order_hbm, grad_hbm, left_prev, right_prev,
    precond_in, left_root_hbm, right_root_hbm, left_stat_hbm, right_stat_hbm, norm_hbm,
    grad, outgoing, owned, left_old, right_old, left_new, right_new,
    left, right, precond, left_in, right_in, ready, packed, packed_in, turned, crossed, doubled,
    high, low, other_high, other_low, factor, square, fourth, iterate, root,
    norm, norm_group, norm_all, norm_pre, norm_train, order, place,
    in_sems, out_sems, send_sems, recv_grad, recv_sems,
    cross_send, cross_recv, norm_send, norm_recv,
):
    me, group = lax.axis_index("train"), lax.axis_index("pre")
    n, groups = lax.axis_size("train"), lax.axis_size("pre")
    blocks, rows, width = grad.shape
    plane, y_at, core_at = me // SUBS, (me // 2) % 2, me % 2
    pair, upper_plane, peers = plane // 2, plane % 2, n // PAIRS
    tile = width // PAIRS

    barrier = pltpu.get_barrier_semaphore()

    load_left = pltpu.make_async_copy(left_prev, left_old, in_sems.at[1])
    load_right = pltpu.make_async_copy(right_prev, right_old, in_sems.at[2])
    load_order = pltpu.make_async_copy(order_hbm, order, in_sems.at[3])
    load_order.start()
    load_grad = copy_in_parts(grad_hbm, grad, in_sems.at[pl.ds(4, 4)])
    load_left.start()
    load_right.start()
    def greet_train(k, _):
        pl.semaphore_signal(
            barrier, inc=1, device_id={"train": (me + k) % n}, device_id_type=MESH
        )
        return 0

    def greet_pre(k, _):
        pl.semaphore_signal(
            barrier, inc=1, device_id={"pre": (group + k) % groups}, device_id_type=MESH
        )
        return 0

    lax.fori_loop(1, n, greet_train, 0)

    @pl.when(me == 0)
    def _():
        lax.fori_loop(1, groups, greet_pre, 0)

    load_order.wait()
    for load in load_grad:
        load.wait()

    def pick(slot, _):
        outgoing[slot] = grad[order[0, slot]]
        return 0

    lax.fori_loop(0, n, pick, 0)
    pl.semaphore_wait(barrier, n - 1 + jnp.where(me == 0, groups - 1, 0))

    def away(step, core):
        return (RINGS - step) // 2 * (2 * (step % 2) - 1) * (1 - 2 * core)

    def device_at(dz, sub):
        z = (plane + dz + RINGS) % RINGS
        return (z * 2 + (y_at + sub // 2) % 2) * 2 + (core_at + sub) % 2

    def push(source, target, send_sem, recv_sem, other):
        pltpu.make_async_remote_copy(
            src_ref=source,
            dst_ref=target,
            send_sem=send_sem,
            recv_sem=recv_sem,
            device_id={"train": other},
            device_id_type=MESH,
        ).start()

    def send_grad(core, half, step):
        across = (half + step) % 2
        other_core = (core_at + core) % 2
        other = device_at(away(step, core_at), 2 * across + other_core)
        at = half * (n // 2) + 2 * step + 1 - other_core

        @pl.when(other != me)
        def _():
            push(outgoing.at[other], owned.at[at], send_sems.at[0], recv_grad.at[half], other)

    def grad_sender(slot):
        half, step, other_core = slot // (n // 2), slot % (n // 2) // 2, 1 - slot % 2
        dz = away(step, (core_at + other_core) % 2)
        return device_at(-dz, 2 * ((half + step) % 2) + other_core)

    def send_part(source, target, which, first, last):
        def send(k, _):
            step = k % RINGS
            other = device_at(away(step, core_at), (step + k // RINGS + 2) % SUBS)
            push(source.at[other], target.at[me], send_sems.at[which], recv_sems.at[which], other)
            return 0

        lax.fori_loop(first, last, send, 0)

    def columns(which_pair):
        return pl.ds(pl.multiple_of(lax.rem(which_pair, PAIRS) * tile, tile), tile)

    sign = 1 - 2 * upper_plane
    span = SUBS * rows

    def lanes(count, size):
        return lax.broadcasted_iota(jnp.int32, (count, tile), 1) // size

    def send_root(source, target, which):
        send_sem, recv_sem = send_sems.at[which], recv_sems.at[which]
        opposite = (plane + RINGS // 2) % RINGS * SUBS
        across = (plane + 3 * sign + RINGS) % RINGS * SUBS
        next_pair = pair + PAIRS + sign
        def send(k, _):
            step = k % 5
            dz = (5 - step) // 2 * (1 - 2 * (step % 2)) * sign
            other = device_at(dz, (step + k // 5 + 1) % SUBS)
            push(source.at[other], target.at[me], send_sem, recv_sem, other)
            return 0

        def send_packed(place, _):
            for kind, first in ((0, opposite), (SUBS, across)):
                push(
                    packed.at[which - 1, kind + place], packed_in.at[which - 1, kind + me % SUBS],
                    send_sem, recv_sem, first + place,
                )
            return 0

        def send_tile(other, at):
            push(source.at[other, :, at], target.at[me, :, at], send_sem, recv_sem, other)

        def send_three(k, _):
            other = (plane - 3 * sign + RINGS) % RINGS * SUBS + k // (PAIRS - 1)
            send_tile(other, columns(pair + PAIRS + 2 * upper_plane + k % (PAIRS - 1)))
            return send(k, 0)

        def send_two(k, _):
            for at in (pair + 2, next_pair + 2):
                send_tile(across + k, columns(at))
            return send(three + k, 0)

        three = SUBS * (PAIRS - 1)
        lax.fori_loop(0, three, send_three, 0)
        for place in range(SUBS):
            ours = source[across + place, :, columns(pair)]
            theirs = source[across + place, :, columns(next_pair)]
            packed[which - 1, SUBS + place] = jnp.where(
                lanes(rows, span) == upper_plane, ours, theirs
            )
            ours = source[opposite + place, :, columns(pair)]
            theirs = pltpu.roll(source[opposite + place, :, columns(pair + 2)], span, 1)
            packed[which - 1, place] = jnp.where(lanes(rows, span) == upper_plane, ours, theirs)
        lax.fori_loop(0, SUBS, send_packed, 0)
        lax.fori_loop(0, SUBS, send_two, 0)
        lax.fori_loop(three + SUBS, n - three - 1, send, 0)
        target[me] = source[me]

    root_chunks = n - 3 * SUBS - 1 + 7 * SUBS // PAIRS

    ring = (3, -3, 2, -2, 1, -1)

    def wrapped(z):
        return lax.rem(z + RINGS, RINGS)

    def exchange(target, which):
        def give(k, to, owners):
            to, owners = wrapped(to), wrapped(owners)
            at = columns(lax.div(to, 2))
            held = target[pl.ds(owners * SUBS, SUBS), :, at].reshape(span, tile)
            doubled[:span], doubled[span:] = held, held
            both = doubled[...].T
            part = jnp.where(lax.rem(to, 2) == 1, both[span:], both[:span])
            part = part.reshape(SUBS, 2, rows // 2, tile)
            first = (lanes(rows // 2, span) == 0)[None]
            turned[which, k] = jnp.where(first, part[:, 0], part[:, 1])

            def send(place, _):
                push(
                    turned.at[which, k, place], crossed.at[which, k, me % SUBS],
                    cross_send.at[which], cross_recv.at[which], to * SUBS + place,
                )
                return 0

            lax.fori_loop(0, SUBS, send, 0)

        for k, dz in enumerate(ring):
            give(k, plane + dz, plane + dz + RINGS // 2)
        give(6, plane + 2 * sign, plane - sign)
        give(7, plane - sign, plane + 2 * sign)
        give(8, plane - 2 * sign, plane + sign)
        give(9, plane + sign, plane - 2 * sign)

    def place_crossed(target, which):
        arrived = crossed.at[which]
        pltpu.make_async_copy(arrived, arrived, cross_recv.at[which]).wait()
        opposite, beside = wrapped(plane + RINGS // 2), wrapped(plane - 3 * sign)
        across = wrapped(plane + 3 * sign)
        missing = columns(pair + 3 + 2 * upper_plane)
        halfway = rows // 2
        mine = lanes(rows, span) == upper_plane
        for block in range(SUBS):
            target[opposite * SUBS + block] = jnp.zeros((rows, width), jnp.float32)
            target[beside * SUBS + block, :, missing] = jnp.zeros((rows, tile), jnp.float32)
            direct = packed_in[which, block]
            for at, values in ((pair + 2, direct), (pair, pltpu.roll(direct, span, 1))):
                target[opposite * SUBS + block, :, columns(at)] = jnp.where(mine, values, 0.0)
            direct = packed_in[which, SUBS + block]
            where = across * SUBS + block
            target[where, :, columns(pair)] = jnp.where(mine, direct, 0.0)
            target[where, :, columns(pair + PAIRS + sign)] = jnp.where(mine, 0.0, direct)

        def take(k, giver, owners):
            giver = wrapped(giver)
            at, odd = columns(lax.div(giver, 2)), lax.rem(giver, 2)
            pieces = [crossed[which, k, sender] for sender in range(SUBS)]
            for block in range(SUBS):
                where = owners * SUBS + block
                top, bottom = target[where, :halfway, at], target[where, halfway:, at]
                for sender in range(SUBS):
                    shift = rows * ((sender - block) % (2 * SUBS))
                    near, far = (
                        pltpu.roll(pieces[sender], by, 1) if by else pieces[sender]
                        for by in (shift, (shift + span) % tile)
                    )
                    here = lanes(halfway, rows) == SUBS * odd + sender
                    top = jnp.where(here, jnp.where(odd == 1, far, near), top)
                    bottom = jnp.where(here, jnp.where(odd == 1, near, far), bottom)
                target[where, :halfway, at] = top
                target[where, halfway:, at] = bottom

        for k, dz in enumerate(ring):
            take(k, plane - dz, opposite)
        take(6, plane - 2 * sign, beside)
        take(7, plane - sign, beside)
        take(8, plane + 2 * sign, across)
        take(9, plane + sign, across)

    def wait_bytes(ref, sem, count=n - 1):
        some = ref.at[pl.ds(0, count)]
        pltpu.make_async_copy(some, some, sem).wait()

    def send_mixed(half, first, k, _):
        for step in range(4):
            send_grad(0, half, 4 * k + step)
        send_grad(1, 0, first + k)
        return 0

    lax.fori_loop(0, 2, functools.partial(send_mixed, 0, 0), 0)
    lax.fori_loop(0, 2, functools.partial(send_mixed, 1, 2), 0)
    for half, first in ((0, 4), (1, 0)):

        def send_rest(step, _):
            send_grad(1, half, step)
            return 0

        lax.fori_loop(first, RINGS, send_rest, 0)
    owned[n - 1] = outgoing[me]

    def invert(block, _):
        def look(slot, found):
            return jnp.where(order[0, slot] == block, slot, found)

        place[block] = lax.fori_loop(0, n, look, 0)
        return 0

    lax.fori_loop(0, blocks, invert, 0)
    grad_sum = total(jnp.sum(grad[...] * grad[...], axis=0))

    def whole(values, count=n):
        return values.reshape(count * rows, width)

    def gram_of(half):
        count = n // 2
        some_high, some_low = split(whole(owned[half * count : (half + 1) * count], count))
        turned_high, turned_low = some_high.T, some_low.T
        for part in halves(width):
            cross = dot(turned_high, some_low[:, part]) + dot(turned_low, some_high[:, part])
            yield part, dot(turned_high, some_high[:, part]) + cross

    def keep_stat(stat, parts):
        squares = jnp.zeros((1, width // 2), jnp.float32)
        for part, values in parts:
            stat[:, part] = values
            squares += jnp.sum(values * values, axis=0, keepdims=True)
        return jnp.sum(squares, axis=1, keepdims=True)

    def put_root(stat, squares, target):
        def finish(part, values):
            target[:, :, part] = values.reshape(n, rows, width // 2)

        inverse_root(stat, squares, factor, square, fourth, iterate, root, finish)

    load_right.wait()
    wait_bytes(owned, recv_grad.at[0], n // 2)
    for part, gram in gram_of(0):
        right_new[:, part] = DECAY * right_old[:, part] + (1.0 - DECAY) * gram
    wait_bytes(owned.at[pl.ds(n // 2, n // 2)], recv_grad.at[1], n // 2 - 1)
    squares = keep_stat(
        right_new,
        [
            (part, right_new[:, part] + (1.0 - DECAY) * gram)
            for part, gram in gram_of(1)
        ],
    )
    store_right_stat = pltpu.make_async_copy(right_new, right_stat_hbm, out_sems.at[1])
    store_right_stat.start()
    put_root(right_new, squares, right)
    send_root(right, right_in, 1)

    def place_rows(k, _):
        at = pl.ds(pl.multiple_of(grad_sender(k) * rows, rows), rows)
        high[at], low[at] = split(owned[k])
        return 0

    lax.fori_loop(0, n, place_rows, 0)
    load_left.wait()
    parts = []
    for part in halves(width):
        gram = dot_t(high[...], high[part]) + (
            dot_t(high[...], low[part]) + dot_t(low[...], high[part])
        )
        parts.append((part, DECAY * left_old[:, part] + (1.0 - DECAY) * gram))
    squares = keep_stat(left_new, parts)
    store_left_stat = pltpu.make_async_copy(left_new, left_stat_hbm, out_sems.at[0])
    store_left_stat.start()
    put_root(left_new, squares, left)

    def keep_split(part, values):
        right_old[:, part] = values

    other_high[...], other_low[...] = split(whole(right[...]))
    product_full(high, low, other_high, other_low, keep_split)
    high[...], low[...] = split(right_old[...])
    other_high[...], other_low[...] = split(whole(left[...]))

    def keep_precond(part, values):
        precond[:, :, part] = values.reshape(n, rows, width // 2)

    product_full(other_high, other_low, high, low, keep_precond)
    prec_sum = total(jnp.sum(precond[...] * precond[...], axis=0))
    upper = lax.broadcasted_iota(jnp.int32, norm.shape, 0) < 4
    norm[...] = jnp.where(upper, grad_sum, prec_sum)

    def share(source, target, which, device):
        pltpu.make_async_remote_copy(
            src_ref=source,
            dst_ref=target,
            send_sem=norm_send.at[which],
            recv_sem=norm_recv.at[which],
            device_id=device,
            device_id_type=MESH,
        ).start()

    def share_pre(k, _):
        share(norm_group, norm_pre.at[group], 1, {"pre": (group + k) % groups})
        return 0

    def share_train(k, _):
        share(norm_all, norm_all, 2, {"train": k})
        return 0

    @pl.when(me != 0)
    def _():
        share(norm, norm_train.at[me], 0, {"train": 0})

    send_root(left, left_in, 2)

    @pl.when(me == 0)
    def _():
        norm_train[0] = norm[...]
        wait_bytes(norm_train, norm_recv.at[0])
        norm_group[...] = jnp.sum(norm_train[...], axis=0)
        lax.fori_loop(1, groups, share_pre, 0)
        norm_pre[group] = norm_group[...]

    wait_bytes(right_in, recv_sems.at[1], root_chunks)
    exchange(right_in, 0)
    send_part(precond, precond_in, 3, 0, n * 9 // 16)

    @pl.when(me == 0)
    def _():
        wait_bytes(norm_pre, norm_recv.at[1], groups - 1)
        wait_bytes(norm_pre, norm_send.at[1], groups - 1)
        norm_all[...] = jnp.sum(norm_pre[...], axis=0)
        lax.fori_loop(1, n, share_train, 0)

    wait_bytes(left_in, recv_sems.at[2], root_chunks)
    exchange(left_in, 1)
    send_part(precond, precond_in, 3, n * 9 // 16, n - 1)
    keep_own = pltpu.make_async_copy(precond.at[me], precond_in.at[me], out_sems.at[4])
    keep_own.start()

    def to_blocks(source, target, which):
        def move(block, _):
            ready[which, block] = source[place[block]]
            return 0

        lax.fori_loop(0, blocks, move, 0)
        store = pltpu.make_async_copy(ready.at[which], target, out_sems.at[2 + which])
        store.start()
        return store

    place_crossed(right_in, 0)
    store_right = to_blocks(right_in, right_root_hbm, 1)
    place_crossed(left_in, 1)
    store_left = to_blocks(left_in, left_root_hbm, 0)

    @pl.when(me != 0)
    def _():
        pltpu.make_async_copy(norm, norm, norm_send.at[0]).wait()
        pltpu.make_async_copy(norm_all, norm_all, norm_recv.at[2]).wait()

    @pl.when(me == 0)
    def _():
        wait_bytes(norm_train, norm_send.at[2])

    store_norm = pltpu.make_async_copy(norm_all, norm_hbm, out_sems.at[5])
    store_norm.start()
    wait_bytes(owned, send_sems.at[0])
    wait_bytes(right, send_sems.at[1], root_chunks)
    wait_bytes(left, send_sems.at[2], root_chunks)
    for which in range(2):
        pltpu.make_async_copy(turned.at[which], turned.at[which], cross_send.at[which]).wait()
    wait_bytes(precond, send_sems.at[3])
    store_left_stat.wait()
    store_right_stat.wait()
    store_left.wait()
    store_right.wait()
    store_norm.wait()
    keep_own.wait()
    wait_bytes(precond_in, recv_sems.at[3])


def in_hbm(value):
    return pltpu.with_memory_space_constraint(value, pltpu.HBM)


def copy_in_parts(source, target, sems):
    count = source.shape[0] // 4
    parts = [pl.ds(part * count, count) for part in range(4)]
    copies = [
        pltpu.make_async_copy(source.at[at], target.at[at], sems.at[part])
        for part, at in enumerate(parts)
    ]
    for copy in copies:
        copy.start()
    return copies


def deliver(
    order_hbm, precond_hbm, left, right, left_stat, right_stat, norm_hbm,
    update, left_out, right_out, left_stat_out, right_stat_out,
    precond, norm, order, in_sems, out_sems,
):
    blocks = precond.shape[0]
    load_order = pltpu.make_async_copy(order_hbm, order, in_sems.at[4])
    load_norm = pltpu.make_async_copy(norm_hbm, norm, in_sems.at[5])
    load_order.start()
    load_norm.start()
    loads = copy_in_parts(precond_hbm, precond, in_sems)
    pairs = ((left, left_out), (right, right_out), (left_stat, left_stat_out), (right_stat, right_stat_out))
    stores = []
    for i, (source, target) in enumerate(pairs):
        stores.append(pltpu.make_async_copy(source, target, out_sems.at[i]))
        stores[-1].start()
    load_order.wait()
    load_norm.wait()
    graft = jnp.sqrt(norm[0:1, 0:1] / (norm[4:5, 0:1] + 1e-6))

    def scale(slot, _):
        precond[slot] = precond[slot] * graft
        pltpu.make_async_copy(
            precond.at[slot], update.at[order[0, slot]], out_sems.at[16]
        ).start()
        return 0

    for part, load in enumerate(loads):
        load.wait()
        lax.fori_loop(part * (blocks // 4), (part + 1) * (blocks // 4), scale, 0)
    for store in stores:
        store.wait()
    pltpu.make_async_copy(precond, update, out_sems.at[16]).wait()


def shards(gradient, assignment, left_prev, right_prev):
    n, groups = lax.axis_size("train"), lax.axis_size("pre")
    blocks, rows, width = gradient.shape
    pieces = jax.ShapeDtypeStruct((blocks, rows, width), jnp.float32)
    square = jax.ShapeDtypeStruct((width, width), jnp.float32)
    any_space = pl.BlockSpec(memory_space=pl.ANY)
    pieces_vmem = pltpu.VMEM(pieces.shape, jnp.float32)
    square_vmem = pltpu.VMEM(square.shape, jnp.float32)
    square_half = pltpu.VMEM(square.shape, jnp.bfloat16)
    results = (pieces, pieces, pieces, square, square)
    made = pl.pallas_call(
        body,
        out_shape=results + (jax.ShapeDtypeStruct((8, 128), jnp.float32),),
        in_specs=[pl.BlockSpec(memory_space=pltpu.HBM)] * 4,
        out_specs=(any_space,) * 6,
        scratch_shapes=[pieces_vmem] * 3
        + [square_vmem] * 4
        + [pieces_vmem] * 5
        + [
            pltpu.VMEM((2,) + pieces.shape, jnp.float32),
            pltpu.VMEM((2, 2 * SUBS, rows, width // PAIRS), jnp.float32),
            pltpu.VMEM((2, 2 * SUBS, rows, width // PAIRS), jnp.float32),
            pltpu.VMEM((2, 10, SUBS, rows // 2, width // PAIRS), jnp.float32),
            pltpu.VMEM((2, 10, SUBS, rows // 2, width // PAIRS), jnp.float32),
            pltpu.VMEM((width // PAIRS, width // PAIRS), jnp.float32),
        ]
        + [square_half] * 4
        + [
            pltpu.VMEM((ITERS,) + square.shape, jnp.bfloat16),
            square_half,
            square_half,
            pltpu.VMEM((ITERS - 1,) + square.shape, jnp.bfloat16),
            pltpu.VMEM((ITERS - 1,) + square.shape, jnp.bfloat16),
            pltpu.VMEM((8, 128), jnp.float32),
            pltpu.VMEM((8, 128), jnp.float32),
            pltpu.VMEM((8, 128), jnp.float32),
            pltpu.VMEM((groups, 8, 128), jnp.float32),
            pltpu.VMEM((n, 8, 128), jnp.float32),
            pltpu.SMEM((1, blocks), jnp.int32),
            pltpu.SMEM((blocks,), jnp.int32),
            pltpu.SemaphoreType.DMA((8,)),
            pltpu.SemaphoreType.DMA((6,)),
            pltpu.SemaphoreType.DMA((4,)),
            pltpu.SemaphoreType.DMA((2,)),
            pltpu.SemaphoreType.DMA((4,)),
            pltpu.SemaphoreType.DMA((2,)),
            pltpu.SemaphoreType.DMA((2,)),
            pltpu.SemaphoreType.DMA((3,)),
            pltpu.SemaphoreType.DMA((3,)),
        ],
        compiler_params=pltpu.CompilerParams(
            collective_id=0, has_side_effects=True, vmem_limit_bytes=48 * 2**20
        ),
        cost_estimate=pl.CostEstimate(
            flops=2 * 28 * width**3, bytes_accessed=32 * width**2, transcendentals=0
        ),
        name="shampoo",
    )(*(in_hbm(value) for value in (assignment, gradient, left_prev[0, 0], right_prev[0, 0])))
    update, left_root, right_root, left_stat, right_stat = pl.pallas_call(
        deliver,
        out_shape=results,
        in_specs=[any_space] * 7,
        out_specs=(pl.BlockSpec(memory_space=pltpu.HBM),) * 5,
        scratch_shapes=[
            pieces_vmem,
            pltpu.VMEM((8, 128), jnp.float32),
            pltpu.SMEM((1, blocks), jnp.int32),
            pltpu.SemaphoreType.DMA((6,)),
            pltpu.SemaphoreType.DMA((17,)),
        ],
        compiler_params=pltpu.CompilerParams(vmem_limit_bytes=4 * 2**20),
        name="deliver",
    )(in_hbm(assignment), *made)
    return update, left_root, right_root, left_stat[None, None], right_stat[None, None]


def solution(mesh):
    by_rows = P("pre", "train", None)
    by_owner = P("pre", "train", None, None)
    return jax.shard_map(
        shards,
        mesh=mesh,
        in_specs=(by_rows, P("pre", None), by_owner, by_owner),
        out_specs=(by_rows, by_rows, by_rows, by_owner, by_owner),
        check_vma=False,
    )
```
